128 devices in a mesh: band: 4 (over z_hi, core), dom: 32 (over z_lo, y, x).
Axes of the slice: x: 4, y: 4, z: 4 (z_hi: 2, z_lo: 2; z = z_hi * 2 + z_lo), core: 2. Of those that a mesh axis runs over, the one named last changes fastest.
Arguments:
- orbitals: float32 [8, 256, 512, 512], P('band', 'dom'), may hold values from -6 to 6
- occupation: int32 [8], P('band'), may hold values from 500 to 2000
- core_density: float32 [256, 512, 512], P('dom', 'band'), may hold values from 0.05 to 0.5
- proj_values: float32 [2048, 8, 128], P('dom'), may hold values from -1.5 to 1.5
- block_index: int32 [2048, 128], P('dom'), may hold values from 0 to 2097151, as said below
- live_points: int32 [2048], P('dom'), may hold values from 32 to 128
Outputs:
- potential: float32 [256, 512, 512], P('dom', 'band')
The draws below stay inside these ranges and needn't reach their ends.
Inputs may be any that keep to these rules, and one draw needn't show every extreme that they name: `block_index`: a flat index into any of the 2097152 cells of the block's own domain.
All inputs are finite; a program needn't handle non-finite values.
Results may differ from the reference program's by a relative error of at most 0.0003.
Values sent between devices are 32-bit elements; how exact they have to be, the bound alone decides.
A program may use at most 128 MiB of HBM per device.

```python
import math
import jax
import jax.numpy as jnp
from jax import lax

CX = 8
NY = 512
NZ = 512
ABLK = 64
PROJ = 8
PTS = 128
ORB = 8
NX = 256
N_DOM = 32


def draw_block_index(key, part):
    key = jax.random.fold_in(key, 11)
    cells = NY * CX * NZ
    rows_all = ABLK * N_DOM
    index = jax.random.randint(key, (rows_all, PTS), 0, cells, dtype=jnp.int32)
    row_ids = lax.broadcasted_iota(jnp.int32, (rows_all, PTS), 0)
    col_ids = lax.broadcasted_iota(jnp.int32, (rows_all, PTS), 1)
    planted = jnp.logical_and(row_ids % ABLK == 0, col_ids == 0)
    return jnp.where(planted, jnp.int32(cells - 1), index).astype(jnp.int32)


def set_ends(values, stream_key, low, largest):
    index_at = [jax.random.randint(jax.random.fold_in(stream_key, axis), (), 0, length) for axis, length in enumerate(values.shape)]
    main_axis = values.shape.index(max(values.shape))
    beside = index_at[:main_axis] + [(index_at[main_axis] + 1) % values.shape[main_axis]] + index_at[main_axis + 1:]
    return values.at[tuple(index_at)].set(low).at[tuple(beside)].set(largest)


def block_levels(own_key, shape, split, low, high):
    def one(axis_at, parts):
        draws = jax.random.uniform(jax.random.fold_in(jax.random.fold_in(own_key, 6), axis_at), (parts,), jnp.float32, low / len(split), high / len(split))
        return jnp.repeat(jnp.exp(draws), shape[axis_at] // parts).reshape((-1,) + (1,) * (len(shape) - axis_at - 1))

    level = one(*split[0])
    for cut in split[1:]:
        level = level * one(*cut)
    return level


def noise(key, dims, spread, reach, pieces=(), held_as=jnp.bfloat16):
    entries = jax.random.normal(key, dims, jnp.float32) * spread
    if len(pieces) > 0:
        entries = block_levels(key, dims, pieces, -0.22, 0.18) * entries
    return jnp.clip(entries, min=-reach, max=reach).astype(held_as)


def setup_inputs(seed: int = 0) -> dict:
    keys = jax.random.split(jax.random.key(seed), 7)
    return {
        "orbitals": noise(keys[0], (ORB, NX, NY, NZ), 1.0, 6.0, ((0, 4), (1, 32)), jnp.float32),
        "occupation": set_ends(jax.random.randint(keys[1], (ORB,), 500, 2001), jax.random.fold_in(keys[1], 1), 500, 2000).astype(jnp.int32),
        "core_density": jnp.clip(0.05 + 0.45 * jax.random.uniform(keys[2], (NX, NY, NZ), jnp.float32) ** block_levels(keys[2], (NX, NY, NZ), ((0, 32), (1, 4)), -0.2, 0.2), 0.05, 0.5),
        "proj_values": noise(keys[3], (ABLK * N_DOM, PROJ, PTS), 0.25, 1.5, ((0, 32),), jnp.float32),
        "block_index": draw_block_index(jax.random.fold_in(keys[6], 71), 0),
        "live_points": set_ends(jax.random.randint(keys[5], (ABLK * N_DOM,), 32, 129), jax.random.fold_in(keys[5], 1), 32, 128).astype(jnp.int32),
    }


coef_a = 0.75 * (3.0 / math.pi) ** (1.0 / 3.0)
kappa_val = 0.804
mu_val = 0.2195149727645171
s_scale = 4.0 * (3.0 * math.pi ** 2) ** (2.0 / 3.0)

def energy_density(density, sigma):
    n_four = density * jnp.cbrt(density)
    reduced = sigma / (s_scale * n_four * n_four)
    factor = 1.0 + kappa_val - kappa_val / (1.0 + mu_val * reduced / kappa_val)
    return -coef_a * n_four * factor

def xc_parts(density, sigma):
    _, pull = jax.vjp(energy_density, density, sigma)
    return pull(jnp.ones_like(density))

def central(field, axis):
    return (jnp.roll(field, -1, axis) - jnp.roll(field, 1, axis)) * 0.5

def reference(orbitals, occupation, core_density, proj_values, block_index, live_points):
    weights = occupation.astype(jnp.float32) * 0.001
    valence = jnp.zeros(orbitals.shape[1:], jnp.float32)
    for orbit in range(ORB):
        valence = valence + weights[orbit] * orbitals[orbit] * orbitals[orbit]
    point_ids = lax.broadcasted_iota(jnp.int32, (ABLK, PTS), 1)

    def slab_augment(dom_id):
        slab = lax.dynamic_slice_in_dim(orbitals, (dom_id * CX).astype(jnp.int32), CX, 1)
        flat = slab.reshape(ORB, CX * NY * NZ)
        first = (dom_id * ABLK).astype(jnp.int32)
        index = lax.dynamic_slice_in_dim(block_index, first, ABLK, 0)
        live = lax.dynamic_slice_in_dim(live_points, first, ABLK, 0)
        values = lax.dynamic_slice_in_dim(proj_values, first, ABLK, 0)
        mask = (point_ids < live[:, None]).astype(jnp.float32)
        beta = values * mask[:, None, :]
        picked = flat[:, index]
        coeff = jnp.einsum('obk,bpk->obp', picked, beta, precision=lax.Precision.HIGHEST)
        strength = jnp.einsum('o,obp->bp', weights, coeff * coeff, precision=lax.Precision.HIGHEST)
        at_points = jnp.einsum('bp,bpk->bk', strength, beta * beta, precision=lax.Precision.HIGHEST)
        added = jnp.zeros((CX * NY * NZ,), jnp.float32).at[index.reshape(-1)].add(at_points.reshape(-1))
        return added.reshape(CX, NY, NZ)
    slabs = lax.map(slab_augment, jnp.arange(N_DOM, dtype=jnp.int32))
    augment = slabs.reshape(NX, NY, NZ)
    density = valence + augment + core_density
    grad_x = central(density, 0)
    grad_y = central(density, 1)
    grad_z = central(density, 2)
    sigma = grad_y * grad_y + grad_x * grad_x + grad_z * grad_z
    e_n, e_sigma = xc_parts(density, sigma)
    flux_y = 2.0 * e_sigma * grad_y
    flux_x = 2.0 * e_sigma * grad_x
    flux_z = 2.0 * e_sigma * grad_z
    divergence = (jnp.roll(flux_y, -1, 1) - jnp.roll(flux_y, 1, 1) + (jnp.roll(flux_x, -1, 0) - jnp.roll(flux_x, 1, 0))) * 0.5 + (jnp.roll(flux_z, -1, 2) - jnp.roll(flux_z, 1, 2)) * 0.5
    return e_n - divergence
```

```python
import functools
import math

import jax
import jax.numpy as jnp
from jax import lax
from jax.experimental import pallas as pl
from jax.experimental.pallas import tpu as pltpu
from jax.sharding import PartitionSpec as P

f32 = jnp.float32
bf16 = jnp.bfloat16
i32 = jnp.int32

coef_a = 0.75 * (3.0 / math.pi) ** (1.0 / 3.0)
kappa_val = 0.804
mu_val = 0.2195149727645171
s_scale = 4.0 * (3.0 * math.pi**2) ** (2.0 / 3.0)

MIB = 2**20
GROUP = 264
LOW = 256
HIGH = 260
ACC_ROWS = 16 * GROUP
N_ACC = 8
NT = (((1,), (1,)), ((), ()))
VM = pl.BlockSpec(memory_space=pltpu.VMEM)
SM = pl.BlockSpec(memory_space=pltpu.SMEM)
ANY = pl.BlockSpec(memory_space=pl.ANY)


def params(mib):
    return pltpu.CompilerParams(vmem_limit_bytes=mib * MIB)


def valence_kernel(place, weights, orb_ref, core_ref, keep_ref, send_ref):
    band = place[0]
    parity = place[1]
    z_hi = place[2]
    w0 = weights[0]
    w1 = weights[1]

    def squares(row, count):
        a = orb_ref[0, 0, pl.ds(row, count), :]
        b = orb_ref[1, 0, pl.ds(row, count), :]
        return w0 * a * a + w1 * b * b

    def plane(i):
        for near in range(2):
            for ref, par in ((keep_ref, parity), (send_ref, 1 - parity)):
                q = 2 * jnp.where(near == 1, z_hi, 1 - z_hi) + par
                for part in range(2):
                    row = pl.multiple_of(q * 128 + 64 * part, 64)
                    own = jnp.where(q == band, 1.0, 0.0)
                    ref[near, 0, pl.ds(128 * i + 64 * part, 64), :] = (
                        squares(row, 64) + own * core_ref[0, 64 * part : 64 * part + 64, :]
                    )
                q_low = (q + 3) % 4
                own = jnp.where(q_low == band, 1.0, 0.0)
                tile = squares(pl.multiple_of(q_low * 128 + 120, 8), 8) + own * core_ref[0, 120:128, :]
                ref[near, 0, pl.ds(LOW + 2 * i, 2), :] = tile[6:8]
                q_high = (q + 1) % 4
                own = jnp.where(q_high == band, 1.0, 0.0)
                tile = squares(pl.multiple_of(q_high * 128, 8), 8) + own * core_ref[0, 0:8, :]
                ref[near, 0, pl.ds(HIGH + 2 * i, 2), :] = tile[0:2]

    for i in range(2):
        pl.when(pl.program_id(0) % 2 == i)(functools.partial(plane, i))


def valence(place, weights, orbitals, core, planes, name):
    first, second = planes

    def plane_of(s):
        return jnp.where(s < 2, first + s, second + s - 2)

    out = jax.ShapeDtypeStruct((2, 2, GROUP, 512), f32)
    return pl.pallas_call(
        valence_kernel,
        grid=(4,),
        in_specs=[
            SM,
            SM,
            pl.BlockSpec((2, 1, 512, 512), lambda s: (0, plane_of(s), 0, 0)),
            pl.BlockSpec((1, 128, 512), lambda s: (plane_of(s), 0, 0)),
        ],
        out_specs=[pl.BlockSpec((2, 1, GROUP, 512), lambda s: (0, s // 2, 0, 0))] * 2,
        out_shape=[out, out],
        compiler_params=params(24),
        cost_estimate=pl.CostEstimate(flops=8 * MIB, bytes_accessed=13 * MIB, transcendentals=0),
        name=name,
    )(place, weights, orbitals, core)


def gather_kernel(weights, rows, lanes, beta, orb, w_ref, buf, picked, sem):
    copies = []
    for o in range(2):
        for x in range(8):
            for c in range(4):
                copy = pltpu.make_async_copy(
                    orb.at[o, x, :, :, pl.ds(128 * c, 128)],
                    buf.at[pl.ds((x * 4 + c) * 64, 64), o],
                    sem.at[o * 32 + x * 4 + c],
                )
                copy.start()
                copies.append(copy)
    for copy in copies:
        copy.wait()
    flat = buf.reshape(32768, 128)
    sub = lax.broadcasted_iota(i32, (128, 128), 0)
    eye = sub == lax.broadcasted_iota(i32, (128, 128), 1)
    lane_ids = lax.broadcasted_iota(i32, (8, 128), 1)
    w0 = weights[0]
    w1 = weights[1]

    def block(b, total):
        for k in range(128):
            r = rows[b, k]
            picked[pl.ds(k, 1), :] = flat[pl.ds(r, 1), :]
            picked[pl.ds(128 + k, 1), :] = flat[pl.ds(r + 8, 1), :]
        hot = jnp.where(lanes[pl.ds(b, 1), :] == sub, 1.0, 0.0).astype(bf16)
        g = picked[...]
        g1 = g.astype(bf16)
        rest = g - g1.astype(f32)
        g2 = rest.astype(bf16)
        g3 = (rest - g2.astype(f32)).astype(bf16)
        t = (
            jnp.dot(g1, hot, preferred_element_type=f32)
            + jnp.dot(g2, hot, preferred_element_type=f32)
            + jnp.dot(g3, hot, preferred_element_type=f32)
        )
        be = beta[b]
        p0 = jnp.sum(jnp.where(eye, t[:128], 0.0), axis=0, keepdims=True)
        p1 = jnp.sum(jnp.where(eye, t[128:], 0.0), axis=0, keepdims=True)
        c0 = jnp.sum(be * p0, axis=1, keepdims=True)
        c1 = jnp.sum(be * p1, axis=1, keepdims=True)
        return jnp.where(lane_ids == b, w0 * c0 * c0 + w1 * c1 * c1, total)

    w_ref[...] = lax.fori_loop(0, 64, block, jnp.zeros((8, 128), f32))


def gather(weights, rows, lanes, beta, orbitals):
    return pl.pallas_call(
        gather_kernel,
        in_specs=[SM, SM, VM, VM, ANY],
        out_specs=VM,
        out_shape=jax.ShapeDtypeStruct((8, 128), f32),
        scratch_shapes=[
            pltpu.VMEM((2048, 2, 8, 128), f32),
            pltpu.VMEM((256, 128), f32),
            pltpu.SemaphoreType.DMA((64,)),
        ],
        compiler_params=params(24),
        cost_estimate=pl.CostEstimate(flops=100 * MIB, bytes_accessed=80 * MIB, transcendentals=0),
        name="gather_points",
    )(weights, rows, lanes, beta, orbitals.reshape(2, 8, 64, 8, 512))


def scatter_kernel(
    rows, lanes, beta, s0, s1, s2, s3, keep, recv, far, d0_ref, d3_ref, aug_ref, spread, *accs
):
    for acc in accs:
        acc[...] = jnp.zeros_like(acc)
    strengths = (s0[...] + s1[...]) + (s2[...] + s3[...])
    sub = lax.broadcasted_iota(i32, (128, 128), 0)
    eye = sub == lax.broadcasted_iota(i32, (128, 128), 1)
    lane_ids = lax.broadcasted_iota(i32, (8, 128), 1)

    def block(b, _):
        be = beta[b]
        w = jnp.sum(jnp.where(lane_ids == b, strengths, 0.0), axis=1, keepdims=True)
        at = jnp.sum(w * be * be, axis=0, keepdims=True)
        a1 = at.astype(bf16).astype(f32)
        rest = at - a1
        a2 = rest.astype(bf16).astype(f32)
        a3 = rest - a2
        hot = jnp.where(lanes[pl.ds(b, 1), :] == sub, 1.0, 0.0).astype(bf16)
        total = None
        for part in (a1, a2, a3):
            diag = jnp.where(eye, part, 0.0).astype(bf16)
            term = lax.dot_general(diag, hot, NT, preferred_element_type=f32)
            total = term if total is None else total + term
        spread[...] = total
        for k in range(0, 128, N_ACC):
            at_rows = [rows[b, k + j] for j in range(N_ACC)]
            old = [accs[j][pl.ds(at_rows[j], 1), :] for j in range(N_ACC)]
            for j in range(N_ACC):
                accs[j][pl.ds(at_rows[j], 1), :] = old[j] + spread[pl.ds(k + j, 1), :]
        return 0

    lax.fori_loop(0, 64, block, 0)

    def summed(g, c):
        piece = pl.ds((g * 4 + c) * GROUP, GROUP)
        total = accs[0][piece, :]
        for acc in accs[1:]:
            total = total + acc[piece, :]
        return total

    for at, g, ref in ((0, 0, d0_ref), (1, 3, d3_ref)):
        for c in range(4):
            cols = slice(128 * c, 128 * c + 128)
            ref[:, cols] = (keep[0, at, :, cols] + recv[0, at, :, cols]) + far[at, :, cols] + summed(g, c)
    for at, g in ((0, 1), (1, 2)):
        for c in range(4):
            aug_ref[at, :, 128 * c : 128 * c + 128] = summed(g, c)


def scatter(rows, lanes, beta, strengths, keep, recv, far):
    group = jax.ShapeDtypeStruct((GROUP, 512), f32)
    near = pl.BlockSpec((1, 2, GROUP, 512), lambda s: (1, 0, 0, 0))
    whole2 = lambda *shape: pl.BlockSpec(shape, lambda s: (0,) * len(shape))
    return pl.pallas_call(
        scatter_kernel,
        grid=(1,),
        in_specs=[
            SM,
            whole2(64, 128),
            whole2(64, 8, 128),
            *[whole2(8, 128)] * 4,
            near,
            near,
            whole2(2, GROUP, 512),
        ],
        out_specs=[whole2(GROUP, 512), whole2(GROUP, 512), whole2(2, GROUP, 512)],
        out_shape=[group, group, jax.ShapeDtypeStruct((2, GROUP, 512), f32)],
        scratch_shapes=[pltpu.VMEM((128, 128), f32)] + [pltpu.VMEM((ACC_ROWS + 8, 128), f32)] * N_ACC,
        compiler_params=params(44),
        cost_estimate=pl.CostEstimate(flops=100 * MIB, bytes_accessed=80 * MIB, transcendentals=0),
        name="scatter_points",
    )(rows, lanes, beta, *strengths, keep, recv, far)


def place_group(dens, plane, group, lead=None):
    for i in range(2):
        dens[plane + i, 16:144, :] = group[pl.ds(128 * i, 128), :]
        dens[plane + i, 14:16, :] = group[pl.ds(LOW + 2 * i, 2), :]
        dens[plane + i, 144:146, :] = group[pl.ds(HIGH + 2 * i, 2), :]


def local_parts(dens, x, row, count):
    mid = dens[x, pl.ds(row, count), :]
    gy = (dens[x, pl.ds(row + 1, count), :] - dens[x, pl.ds(row - 1, count), :]) * 0.5
    gx = (dens[x + 1, pl.ds(row, count), :] - dens[x - 1, pl.ds(row, count), :]) * 0.5
    gz = (pltpu.roll(mid, 511, 1) - pltpu.roll(mid, 1, 1)) * 0.5
    sigma = gy * gy + gx * gx + gz * gz
    logs = jnp.log(mid)
    cube = jnp.exp(logs * (1.0 / 3.0))
    inv_four = jnp.exp(logs * (-4.0 / 3.0))
    reduced = sigma * (inv_four * inv_four) * (1.0 / s_scale)
    inv = 1.0 / (1.0 + (mu_val / kappa_val) * reduced)
    slope = mu_val * inv * inv
    factor = (1.0 + kappa_val) - kappa_val * inv
    e_n = (-4.0 / 3.0 * coef_a) * cube * (factor - 2.0 * reduced * slope)
    twice = (-2.0 * coef_a / s_scale) * inv_four * slope
    return e_n, twice * gy, twice * gx, twice * gz


STRIP = 16


def full_plane(dens, x, flux_y, put):
    for row in (8, 144):
        flux_y[pl.ds(row, 8), :] = local_parts(dens, x, row, 8)[1]
    for row in range(16, 144, STRIP):
        e_n, fy, fx, fz = local_parts(dens, x, row, STRIP)
        flux_y[pl.ds(row, STRIP), :] = fy
        put(row - 16, e_n - (pltpu.roll(fz, 511, 1) - pltpu.roll(fz, 1, 1)) * 0.5, fx)


def minus_y(flux_y, row):
    up = flux_y[pl.ds(row + 17, STRIP), :]
    down = flux_y[pl.ds(row + 15, STRIP), :]
    return (up - down) * 0.5


def inner_kernel(d0, d3, keep, recv, far, aug, pot_ref, low_ref, high_ref, dens, flux_x, flux_y):
    place_group(dens, 0, d0)
    place_group(dens, 6, d3)
    for g in range(2):
        total = (keep[0, g] + recv[0, g]) + far[g] + aug[g]
        for i in range(2):
            dens[2 + 2 * g + i, 16:144, :] = total[128 * i : 128 * i + 128]
            dens[2 + 2 * g + i, 14:16, :] = total[LOW + 2 * i : LOW + 2 * i + 2]
            dens[2 + 2 * g + i, 144:146, :] = total[HIGH + 2 * i : HIGH + 2 * i + 2]

    def plane(x, _):
        def put(row, value, fx):
            pot_ref[x, pl.ds(row, STRIP), :] = value
            flux_x[x, pl.ds(row, STRIP), :] = fx

        full_plane(dens, x, flux_y, put)
        for row in range(0, 128, STRIP):
            here = pl.ds(row, STRIP)
            pot_ref[x, here, :] = pot_ref[x, here, :] - minus_y(flux_y, row)
        return 0

    lax.fori_loop(1, 7, plane, 0)

    def across(x, _):
        for row in range(0, 128, STRIP):
            here = pl.ds(row, STRIP)
            pot_ref[x, here, :] = (
                pot_ref[x, here, :] - (flux_x[x + 1, here, :] - flux_x[x - 1, here, :]) * 0.5
            )
        return 0

    lax.fori_loop(2, 6, across, 0)
    pot_ref[1] = pot_ref[1] - flux_x[2] * 0.5
    pot_ref[6] = pot_ref[6] + flux_x[5] * 0.5
    pot_ref[0] = jnp.zeros((128, 512), f32)
    pot_ref[7] = jnp.zeros((128, 512), f32)
    low_ref[...] = flux_x[1]
    high_ref[...] = flux_x[6]


def inner(d0, d3, keep, recv, far, aug):
    near = pl.BlockSpec((1, 2, GROUP, 512), lambda s: (1, 0, 0, 0))
    whole2 = lambda *shape: pl.BlockSpec(shape, lambda s: (0,) * len(shape))
    plane = jax.ShapeDtypeStruct((128, 512), f32)
    return pl.pallas_call(
        inner_kernel,
        grid=(1,),
        in_specs=[whole2(GROUP, 512)] * 2 + [near, near] + [whole2(2, GROUP, 512)] * 2,
        out_specs=[whole2(8, 128, 512), whole2(128, 512), whole2(128, 512)],
        out_shape=[jax.ShapeDtypeStruct((8, 128, 512), f32), plane, plane],
        scratch_shapes=[
            pltpu.VMEM((8, 160, 512), f32),
            pltpu.VMEM((8, 128, 512), f32),
            pltpu.VMEM((160, 512), f32),
        ],
        compiler_params=params(40),
        cost_estimate=pl.CostEstimate(flops=100 * MIB, bytes_accessed=30 * MIB, transcendentals=0),
        name="inner_planes",
    )(d0, d3, keep, recv, far, aug)


def outer_kernel(below, d0, d3, above, old, low, high, pot_ref, dens, flux_x, flux_y):
    place_group(dens, 0, below)
    place_group(dens, 2, d0)
    place_group(dens, 4, d3)
    place_group(dens, 6, above)
    for row in range(0, 128, STRIP):
        flux_x[0, pl.ds(row, STRIP), :] = local_parts(dens, 1, row + 16, STRIP)[2]
        flux_x[1, pl.ds(row, STRIP), :] = local_parts(dens, 6, row + 16, STRIP)[2]

    for end, x, edge, inside in ((0, 2, 0, 1), (1, 5, 3, 2)):

        def put(row, value, fx):
            here = pl.ds(row, STRIP)
            pot_ref[edge, here, :] = value
            if end == 0:
                pot_ref[inside, here, :] = old[1, here, :] + 0.5 * fx
            else:
                pot_ref[inside, here, :] = old[2, here, :] - 0.5 * fx

        full_plane(dens, x, flux_y, put)
        for row in range(0, 128, STRIP):
            here = pl.ds(row, STRIP)
            if end == 0:
                across = (low[here, :] - flux_x[0, here, :]) * 0.5
            else:
                across = (flux_x[1, here, :] - high[here, :]) * 0.5
            pot_ref[edge, here, :] = pot_ref[edge, here, :] - minus_y(flux_y, row) - across


def outer_body(below, d0, d3, above, old_ref, low, high, pot_ref, dens, flux_x, flux_y, old, new, sem):
    ins = [
        pltpu.make_async_copy(old_ref.at[pl.ds(0, 2)], old.at[pl.ds(0, 2)], sem.at[0]),
        pltpu.make_async_copy(old_ref.at[pl.ds(6, 2)], old.at[pl.ds(2, 2)], sem.at[1]),
    ]
    for copy in ins:
        copy.start()
    for copy in ins:
        copy.wait()
    outer_kernel(below, d0, d3, above, old, low, high, new, dens, flux_x, flux_y)
    outs = [
        pltpu.make_async_copy(new.at[pl.ds(0, 2)], pot_ref.at[pl.ds(0, 2)], sem.at[2]),
        pltpu.make_async_copy(new.at[pl.ds(2, 2)], pot_ref.at[pl.ds(6, 2)], sem.at[3]),
    ]
    for copy in outs:
        copy.start()
    for copy in outs:
        copy.wait()


def outer(below, d0, d3, above, old, low, high):
    return pl.pallas_call(
        outer_body,
        in_specs=[VM, VM, VM, VM, ANY, VM, VM],
        out_specs=ANY,
        out_shape=jax.ShapeDtypeStruct((8, 128, 512), f32),
        input_output_aliases={4: 0},
        scratch_shapes=[
            pltpu.VMEM((8, 160, 512), f32),
            pltpu.VMEM((2, 128, 512), f32),
            pltpu.VMEM((160, 512), f32),
            pltpu.VMEM((4, 128, 512), f32),
            pltpu.VMEM((4, 128, 512), f32),
            pltpu.SemaphoreType.DMA((4,)),
        ],
        compiler_params=params(40),
        cost_estimate=pl.CostEstimate(flops=100 * MIB, bytes_accessed=30 * MIB, transcendentals=0),
        name="outer_planes",
    )(below, d0, d3, above, old, low, high)


def shards(orbitals, occupation, core_density, proj_values, block_index, live_points):
    band = lax.axis_index("band")
    place = jnp.stack([band, band % 2, band // 2]).astype(i32)
    weights = occupation.astype(f32) * 0.001

    swap_pairs = [(0, 1), (1, 0), (2, 3), (3, 2)]
    far_pairs = [(0, 2), (2, 0), (1, 3), (3, 1)]

    keep_a, send_a = valence(place, weights, orbitals, core_density, (0, 6), "valence_outer")
    recv_a = lax.ppermute(send_a, "band", swap_pairs)
    keep_b, send_b = valence(place, weights, orbitals, core_density, (2, 4), "valence_inner")
    recv_b = lax.ppermute(send_b, "band", swap_pairs)
    far_a = lax.ppermute(keep_a[0] + recv_a[0], "band", far_pairs)
    far_b = lax.ppermute(keep_b[0] + recv_b[0], "band", far_pairs)

    point_ids = lax.broadcasted_iota(i32, block_index.shape, 1)
    beta = proj_values * (point_ids < live_points[:, None]).astype(f32)[:, None, :]
    x = block_index >> 18
    y = (block_index >> 9) & 511
    c = (block_index >> 7) & 3
    lanes = block_index & 127
    from_rows = ((x * 4 + c) * 64 + (y >> 3)) * 16 + (y & 7)
    own = (y - 128 * band) & 511
    pair = (x & 1) * 2
    inside = jnp.where(
        own < 128,
        (x & 1) * 128 + own,
        jnp.where(own >= 510, LOW + pair + own - 510, HIGH + pair + own - 128),
    )
    into_rows = jnp.where(
        (own < 130) | (own >= 510), ((x >> 1) * 4 + c) * GROUP + inside, ACC_ROWS
    )

    mine = gather(weights, from_rows, lanes, beta, orbitals)
    strengths = [mine] + [
        lax.ppermute(mine, "band", [(i, (i + step) % 4) for i in range(4)]) for step in (1, 2, 3)
    ]
    d0, d3, aug = scatter(into_rows, lanes, beta, strengths, keep_a, recv_a, far_a)
    above = lax.ppermute(d0, "dom", [((i + 1) % 32, i) for i in range(32)])
    below = lax.ppermute(d3, "dom", [(i, (i + 1) % 32) for i in range(32)])
    part, low, high = inner(d0, d3, keep_b, recv_b, far_b, aug)
    return outer(below, d0, d3, above, part, low, high)


def solution(mesh):
    placed = (
        P("band", "dom", None, None),
        P("band"),
        P("dom", "band", None),
        P("dom", None, None),
        P("dom", None),
        P("dom"),
    )
    return jax.shard_map(
        shards, mesh=mesh, in_specs=placed, out_specs=P("dom", "band", None), check_vma=False
    )
```

```python
import functools
import math

import jax
import jax.numpy as jnp
from jax import lax
from jax.experimental import pallas as pl
from jax.experimental.pallas import tpu as pltpu
from jax.sharding import PartitionSpec as P

f32 = jnp.float32
bf16 = jnp.bfloat16
i32 = jnp.int32

coef_a = 0.75 * (3.0 / math.pi) ** (1.0 / 3.0)
kappa_val = 0.804
mu_val = 0.2195149727645171
s_scale = 4.0 * (3.0 * math.pi**2) ** (2.0 / 3.0)
LOG2E = math.log2(math.e)

MIB = 2**20
GROUP = 264
LOW = 256
HIGH = 260
ACC_ROWS = 16 * GROUP
N_ACC = 8
NT = (((1,), (1,)), ((), ()))
VM = pl.BlockSpec(memory_space=pltpu.VMEM)
SM = pl.BlockSpec(memory_space=pltpu.SMEM)
ANY = pl.BlockSpec(memory_space=pl.ANY)
HBM = pl.BlockSpec(memory_space=pltpu.HBM)


def params(mib):
    return pltpu.CompilerParams(vmem_limit_bytes=mib * MIB)


MESH = pl.DeviceIdType.MESH
STEP = 8
ORDER = (0, 3, 1, 2)
TILES = GROUP // 8 * 4


def front_kernel(
    weights, rows, lanes, beta, core, orb,
    w_ref, outer_ref, near_ref, far_ref,
    buf, picked, keep, send, recv, come, w_mine, w_core, w_come,
    load_sem, swap_out, swap_in, far_out, far_in, w_out, w_in,
):
    band = lax.axis_index("band")
    dom = lax.axis_index("dom")
    parity = lax.rem(band, 2)
    z_hi = band // 2
    mate = (band + 1 - 2 * parity, dom)
    opposite = (lax.rem(band + 2, 4), dom)

    def loads(gi):
        made = []
        for i in range(2):
            x = 2 * ORDER[gi] + i
            for o in range(2):
                made.append(
                    pltpu.make_async_copy(
                        orb.at[o, x], buf.at[pl.ds(256 * x, 256), o], load_sem.at[4 * gi + 2 * i + o]
                    )
                )
        return made

    for gi in range(2):
        for copy in loads(gi):
            copy.start()
    barrier = pltpu.get_barrier_semaphore()
    for partner in (mate, opposite):
        pl.semaphore_signal(barrier, inc=1, device_id=partner, device_id_type=MESH)
    w0 = weights[0]
    w1 = weights[1]

    def squares(tile, count):
        a = buf[pl.ds(tile, count), 0]
        b = buf[pl.ds(tile, count), 1]
        return w0 * a * a + w1 * b * b

    def fill(ref, gi, near, mine):
        q = 2 * (z_hi if near else 1 - z_hi) + (parity if mine else 1 - parity)
        for i in range(2):
            x = 2 * ORDER[gi] + i

            def body(j, _):
                value = squares(x * 256 + q * 64 + 16 * j, 16)
                if near and mine:
                    value = value + core[x, pl.ds(16 * j, 16)]
                ref[near, gi, pl.ds(64 * i + 16 * j, 16)] = value
                return 0

            lax.fori_loop(0, 4, body, 0)
            q_low = lax.rem(q + 3, 4)
            own = jnp.where(q_low == band, 1.0, 0.0)
            value = squares(x * 256 + q_low * 64 + 60, 4) + own * core[x, 60:64]
            ref[near, gi, 128:132, 2 * i : 2 * i + 2, :] = value[:, 6:8, :]
            q_high = lax.rem(q + 1, 4)
            own = jnp.where(q_high == band, 1.0, 0.0)
            value = squares(x * 256 + q_high * 64, 4) + own * core[x, 0:4]
            ref[near, gi, 128:132, 4 + 2 * i : 6 + 2 * i, :] = value[:, 0:2, :]

    def swap(near, gi):
        return pltpu.make_async_remote_copy(
            src_ref=send.at[near, gi],
            dst_ref=recv.at[near, gi],
            send_sem=swap_out.at[4 * near + gi],
            recv_sem=swap_in.at[4 * near + gi],
            device_id=mate,
            device_id_type=MESH,
        )

    def across(gi):
        return pltpu.make_async_remote_copy(
            src_ref=keep.at[0, gi],
            dst_ref=come.at[gi],
            send_sem=far_out.at[gi],
            recv_sem=far_in.at[gi],
            device_id=opposite,
            device_id_type=MESH,
        )

    def summed(near, gi, put):
        def body(j, _):
            here = pl.ds(12 * j, 12)
            put(here, keep[near, gi, here] + recv[near, gi, here])
            return 0

        lax.fori_loop(0, TILES // 12, body, 0)

    for gi in range(4):
        for copy in loads(gi):
            copy.wait()
        if gi < 2:
            for copy in loads(gi + 2):
                copy.start()
        fill(send, gi, 0, False)
        if gi == 0:
            pl.semaphore_wait(barrier, 2)
        swap(0, gi).start()
        fill(keep, gi, 0, True)
        fill(send, gi, 1, False)
        swap(1, gi).start()
        fill(keep, gi, 1, True)
        swap(0, gi).wait()

        def put_far(here, value):
            keep[0, gi, here] = value

        def put_out(here, value):
            far_ref[gi - 2, here] = value

        summed(0, gi, put_far if gi < 2 else put_out)
        if gi < 2:
            across(gi).start()

    flat = buf.reshape(32768, 128)
    sub = lax.broadcasted_iota(i32, (128, 128), 0)
    two = lax.broadcasted_iota(i32, (256, 128), 0) - 2 * lax.broadcasted_iota(i32, (256, 128), 1)
    even = two == 0
    odd = two == 1
    lane_ids = lax.broadcasted_iota(i32, (8, 128), 1)

    def step(i, total):
        for j in range(STEP):
            for k in range(128):
                r = rows[STEP * i + j, k]
                picked[pl.ds(256 * j + 2 * k, 2), :] = flat[pl.ds(r, 2, stride=8), :]
        for j in range(STEP):
            b = STEP * i + j
            hot = jnp.where(lanes[pl.ds(b, 1), :] == sub, 1.0, 0.0).astype(bf16)
            g = picked[256 * j : 256 * j + 256]
            g1 = g.astype(bf16)
            g2 = (g - g1.astype(f32)).astype(bf16)
            t = jnp.dot(g1, hot, preferred_element_type=f32) + jnp.dot(g2, hot, preferred_element_type=f32)
            be = beta[b]
            p0 = jnp.sum(jnp.where(even, t, 0.0), axis=0, keepdims=True)
            p1 = jnp.sum(jnp.where(odd, t, 0.0), axis=0, keepdims=True)
            c0 = jnp.sum(be * p0, axis=1, keepdims=True)
            c1 = jnp.sum(be * p1, axis=1, keepdims=True)
            total = jnp.where(lane_ids == b, w0 * c0 * c0 + w1 * c1 * c1, total)
        return total

    w_mine[...] = lax.fori_loop(0, 64 // STEP, step, jnp.zeros((8, 128), f32))

    def send_w(src, dst, at, target):
        return pltpu.make_async_remote_copy(
            src_ref=src,
            dst_ref=dst,
            send_sem=w_out.at[at],
            recv_sem=w_in.at[at],
            device_id=target,
            device_id_type=MESH,
        )

    first = send_w(w_mine, w_come.at[0], 0, mate)
    first.start()
    for gi in range(4):
        swap(1, gi).wait()

        def put_near(here, value):
            near_ref[gi - 2, here] = value

        def put_keep(here, value):
            keep[1, gi, here] = value

        summed(1, gi, put_keep if gi < 2 else put_near)
    first.wait()
    w_core[...] = w_mine[...] + w_come[0]
    second = send_w(w_core, w_come.at[1], 1, opposite)
    second.start()
    for gi in range(2):
        across(gi).wait()

        def body(j, _):
            here = pl.ds(12 * j, 12)
            outer_ref[gi, here] = keep[1, gi, here] + come[gi, here]
            return 0

        lax.fori_loop(0, TILES // 12, body, 0)
    second.wait()
    w_ref[...] = w_core[...] + w_come[1]


def front(weights, rows, lanes, beta, core, orbitals):
    tiles = orbitals.reshape(2, 8, 64, 8, 4, 128).transpose(0, 1, 2, 4, 3, 5).reshape(2, 8, 256, 8, 128)
    core = core.reshape(8, 16, 8, 4, 128).transpose(0, 1, 3, 2, 4).reshape(8, 64, 8, 128)
    pair = jax.ShapeDtypeStruct((2, TILES, 8, 128), f32)
    both = pltpu.VMEM((2, 4, TILES, 8, 128), f32)
    strengths = pltpu.VMEM((8, 128), f32)
    dma = pltpu.SemaphoreType.DMA
    w, outer_sum, near, far = pl.pallas_call(
        front_kernel,
        in_specs=[SM, SM, VM, VM, VM, HBM],
        out_specs=[VM] * 4,
        out_shape=[jax.ShapeDtypeStruct((8, 128), f32), pair, pair, pair],
        scratch_shapes=[
            pltpu.VMEM((2048, 2, 8, 128), f32),
            pltpu.VMEM((256 * STEP, 128), f32),
            both,
            both,
            both,
            pltpu.VMEM((2, TILES, 8, 128), f32),
            strengths,
            strengths,
            pltpu.VMEM((2, 8, 128), f32),
            dma((16,)),
            dma((8,)),
            dma((8,)),
            dma((2,)),
            dma((2,)),
            dma((2,)),
            dma((2,)),
        ],
        compiler_params=pltpu.CompilerParams(
            vmem_limit_bytes=60 * MIB, collective_id=0, has_side_effects=True
        ),
        cost_estimate=pl.CostEstimate(flops=100 * MIB, bytes_accessed=40 * MIB, transcendentals=0),
        name="front",
    )(weights, rows, lanes, beta, core, tiles)
    plain = lambda t: t.reshape(2, 33, 4, 8, 128).transpose(0, 1, 3, 2, 4).reshape(2, GROUP, 512)
    return w, plain(outer_sum), plain(near), plain(far)


def scatter_kernel(
    rows, lanes, beta, strength_ref, sums, d0_ref, d3_ref, aug_ref, spread, *accs
):
    for acc in accs:
        acc[...] = jnp.zeros_like(acc)
    strengths = strength_ref[...]
    sub = lax.broadcasted_iota(i32, (128, 128), 0)
    eye = sub == lax.broadcasted_iota(i32, (128, 128), 1)
    lane_ids = lax.broadcasted_iota(i32, (8, 128), 1)

    def spread_step(i, _):
        for j in range(STEP):
            b = STEP * i + j
            be = beta[b]
            w = jnp.sum(jnp.where(lane_ids == b, strengths, 0.0), axis=1, keepdims=True)
            at = jnp.sum(w * be * be, axis=0, keepdims=True)
            a1 = at.astype(bf16).astype(f32)
            hot = jnp.where(lanes[pl.ds(b, 1), :] == sub, 1.0, 0.0).astype(bf16)
            d1 = jnp.where(eye, a1, 0.0).astype(bf16)
            d2 = jnp.where(eye, at - a1, 0.0).astype(bf16)
            spread[pl.ds(pl.multiple_of(b * 128, 128), 128), :] = lax.dot_general(
                d1, hot, NT, preferred_element_type=f32
            ) + lax.dot_general(d2, hot, NT, preferred_element_type=f32)
        return 0

    lax.fori_loop(0, 64 // STEP, spread_step, 0)

    def add_step(b, _):
        first = pl.multiple_of(b * 128, 128)
        for k in range(0, 128, N_ACC):
            at_rows = [rows[b, k + j] for j in range(N_ACC)]
            old = [accs[j][pl.ds(at_rows[j], 1), :] for j in range(N_ACC)]
            for j in range(N_ACC):
                accs[j][pl.ds(at_rows[j], 1), :] = old[j] + spread[pl.ds(first + k + j, 1), :]
        return 0

    lax.fori_loop(0, 64, add_step, 0)

    def summed(g, c):
        piece = pl.ds((g * 4 + c) * GROUP, GROUP)
        total = accs[0][piece, :]
        for acc in accs[1:]:
            total = total + acc[piece, :]
        return total

    for at, g, ref in ((0, 0, d0_ref), (1, 3, d3_ref)):
        for c in range(4):
            cols = slice(128 * c, 128 * c + 128)
            ref[:, cols] = sums[at, :, cols] + summed(g, c)
    for at, g in ((0, 1), (1, 2)):
        for c in range(4):
            aug_ref[at, :, 128 * c : 128 * c + 128] = summed(g, c)


def scatter(rows, lanes, beta, strengths, sums):
    group = jax.ShapeDtypeStruct((GROUP, 512), f32)
    whole2 = lambda *shape: pl.BlockSpec(shape, lambda s: (0,) * len(shape))
    return pl.pallas_call(
        scatter_kernel,
        grid=(1,),
        in_specs=[
            SM,
            whole2(64, 128),
            whole2(64, 8, 128),
            whole2(8, 128),
            whole2(2, GROUP, 512),
        ],
        out_specs=[whole2(GROUP, 512), whole2(GROUP, 512), whole2(2, GROUP, 512)],
        out_shape=[group, group, jax.ShapeDtypeStruct((2, GROUP, 512), f32)],
        scratch_shapes=[pltpu.VMEM((8192, 128), f32)] + [pltpu.VMEM((ACC_ROWS + 8, 128), f32)] * N_ACC,
        compiler_params=params(60),
        cost_estimate=pl.CostEstimate(flops=100 * MIB, bytes_accessed=80 * MIB, transcendentals=0),
        name="scatter_points",
    )(rows, lanes, beta, strengths, sums)


def place_group(dens, plane, group, lead=None):
    for i in range(2):
        dens[plane + i, 16:144, :] = group[pl.ds(128 * i, 128), :]
        dens[plane + i, 14:16, :] = group[pl.ds(LOW + 2 * i, 2), :]
        dens[plane + i, 144:146, :] = group[pl.ds(HIGH + 2 * i, 2), :]


def local_parts(dens, x, row, count):
    mid = dens[x, pl.ds(row, count), :]
    gy = (dens[x, pl.ds(row + 1, count), :] - dens[x, pl.ds(row - 1, count), :]) * 0.5
    gx = (dens[x + 1, pl.ds(row, count), :] - dens[x - 1, pl.ds(row, count), :]) * 0.5
    gz = (pltpu.roll(mid, 511, 1) - pltpu.roll(mid, 1, 1)) * 0.5
    sigma = gy * gy + gx * gx + gz * gz
    logs = jnp.log(mid)
    cube = jnp.exp2(logs * (LOG2E / 3.0))
    inv_four = jnp.exp2(logs * (-4.0 * LOG2E / 3.0))
    reduced = sigma * (inv_four * inv_four) * (1.0 / s_scale)
    under = 1.0 + (mu_val / kappa_val) * reduced
    inv = pl.reciprocal(under, approx=True)
    inv = inv * (2.0 - under * inv)
    slope = mu_val * inv * inv
    factor = (1.0 + kappa_val) - kappa_val * inv
    e_n = (-4.0 / 3.0 * coef_a) * cube * (factor - 2.0 * reduced * slope)
    twice = (-2.0 * coef_a / s_scale) * inv_four * slope
    return e_n, twice * gy, twice * gx, twice * gz


STRIP = 16


def full_plane(dens, x, flux_y, put):
    for row in (8, 144):
        flux_y[pl.ds(row, 8), :] = local_parts(dens, x, row, 8)[1]
    for row in range(16, 144, STRIP):
        e_n, fy, fx, fz = local_parts(dens, x, row, STRIP)
        flux_y[pl.ds(row, STRIP), :] = fy
        put(row - 16, e_n - (pltpu.roll(fz, 511, 1) - pltpu.roll(fz, 1, 1)) * 0.5, fx)


def minus_y(flux_y, row):
    up = flux_y[pl.ds(row + 17, STRIP), :]
    down = flux_y[pl.ds(row + 15, STRIP), :]
    return (up - down) * 0.5


def inner_kernel(d0, d3, near, far, aug, pot_ref, low_ref, high_ref, dens, flux_x, flux_y):
    place_group(dens, 0, d0)
    place_group(dens, 6, d3)
    for g in range(2):
        total = near[g] + far[g] + aug[g]
        for i in range(2):
            dens[2 + 2 * g + i, 16:144, :] = total[128 * i : 128 * i + 128]
            dens[2 + 2 * g + i, 14:16, :] = total[LOW + 2 * i : LOW + 2 * i + 2]
            dens[2 + 2 * g + i, 144:146, :] = total[HIGH + 2 * i : HIGH + 2 * i + 2]

    def plane(x, _):
        def put(row, value, fx):
            pot_ref[x, pl.ds(row, STRIP), :] = value
            flux_x[x, pl.ds(row, STRIP), :] = fx

        full_plane(dens, x, flux_y, put)
        for row in range(0, 128, STRIP):
            here = pl.ds(row, STRIP)
            pot_ref[x, here, :] = pot_ref[x, here, :] - minus_y(flux_y, row)
        return 0

    lax.fori_loop(1, 7, plane, 0)

    def across(x, _):
        for row in range(0, 128, STRIP):
            here = pl.ds(row, STRIP)
            pot_ref[x, here, :] = (
                pot_ref[x, here, :] - (flux_x[x + 1, here, :] - flux_x[x - 1, here, :]) * 0.5
            )
        return 0

    lax.fori_loop(2, 6, across, 0)
    pot_ref[1] = pot_ref[1] - flux_x[2] * 0.5
    pot_ref[6] = pot_ref[6] + flux_x[5] * 0.5
    pot_ref[0] = jnp.zeros((128, 512), f32)
    pot_ref[7] = jnp.zeros((128, 512), f32)
    low_ref[...] = flux_x[1]
    high_ref[...] = flux_x[6]


def inner(d0, d3, near, far, aug):
    whole2 = lambda *shape: pl.BlockSpec(shape, lambda s: (0,) * len(shape))
    plane = jax.ShapeDtypeStruct((128, 512), f32)
    return pl.pallas_call(
        inner_kernel,
        grid=(1,),
        in_specs=[whole2(GROUP, 512)] * 2 + [whole2(2, GROUP, 512)] * 3,
        out_specs=[whole2(8, 128, 512), whole2(128, 512), whole2(128, 512)],
        out_shape=[jax.ShapeDtypeStruct((8, 128, 512), f32), plane, plane],
        scratch_shapes=[
            pltpu.VMEM((8, 160, 512), f32),
            pltpu.VMEM((8, 128, 512), f32),
            pltpu.VMEM((160, 512), f32),
        ],
        compiler_params=params(60),
        cost_estimate=pl.CostEstimate(flops=100 * MIB, bytes_accessed=30 * MIB, transcendentals=0),
        name="inner_planes",
    )(d0, d3, near, far, aug)


def outer_kernel(below, d0, d3, above, old, low, high, pot_ref, dens, flux_x, flux_y):
    place_group(dens, 0, below)
    place_group(dens, 2, d0)
    place_group(dens, 4, d3)
    place_group(dens, 6, above)
    for row in range(0, 128, STRIP):
        flux_x[0, pl.ds(row, STRIP), :] = local_parts(dens, 1, row + 16, STRIP)[2]
        flux_x[1, pl.ds(row, STRIP), :] = local_parts(dens, 6, row + 16, STRIP)[2]

    for end, x, edge, inside in ((0, 2, 0, 1), (1, 5, 3, 2)):

        def put(row, value, fx):
            here = pl.ds(row, STRIP)
            pot_ref[edge, here, :] = value
            if end == 0:
                pot_ref[inside, here, :] = old[1, here, :] + 0.5 * fx
            else:
                pot_ref[inside, here, :] = old[2, here, :] - 0.5 * fx

        full_plane(dens, x, flux_y, put)
        for row in range(0, 128, STRIP):
            here = pl.ds(row, STRIP)
            if end == 0:
                across = (low[here, :] - flux_x[0, here, :]) * 0.5
            else:
                across = (flux_x[1, here, :] - high[here, :]) * 0.5
            pot_ref[edge, here, :] = pot_ref[edge, here, :] - minus_y(flux_y, row) - across


def outer_body(below, d0, d3, above, old_ref, low, high, pot_ref, dens, flux_x, flux_y, old, new, sem):
    ins = [
        pltpu.make_async_copy(old_ref.at[pl.ds(0, 2)], old.at[pl.ds(0, 2)], sem.at[0]),
        pltpu.make_async_copy(old_ref.at[pl.ds(6, 2)], old.at[pl.ds(2, 2)], sem.at[1]),
    ]
    for copy in ins:
        copy.start()
    for copy in ins:
        copy.wait()
    outer_kernel(below, d0, d3, above, old, low, high, new, dens, flux_x, flux_y)
    outs = [
        pltpu.make_async_copy(new.at[pl.ds(0, 2)], pot_ref.at[pl.ds(0, 2)], sem.at[2]),
        pltpu.make_async_copy(new.at[pl.ds(2, 2)], pot_ref.at[pl.ds(6, 2)], sem.at[3]),
    ]
    for copy in outs:
        copy.start()
    for copy in outs:
        copy.wait()


def outer(below, d0, d3, above, old, low, high):
    return pl.pallas_call(
        outer_body,
        in_specs=[VM, VM, VM, VM, ANY, VM, VM],
        out_specs=ANY,
        out_shape=jax.ShapeDtypeStruct((8, 128, 512), f32),
        input_output_aliases={4: 0},
        scratch_shapes=[
            pltpu.VMEM((8, 160, 512), f32),
            pltpu.VMEM((2, 128, 512), f32),
            pltpu.VMEM((160, 512), f32),
            pltpu.VMEM((4, 128, 512), f32),
            pltpu.VMEM((4, 128, 512), f32),
            pltpu.SemaphoreType.DMA((4,)),
        ],
        compiler_params=params(60),
        cost_estimate=pl.CostEstimate(flops=100 * MIB, bytes_accessed=30 * MIB, transcendentals=0),
        name="outer_planes",
    )(below, d0, d3, above, old, low, high)


def shards(orbitals, occupation, core_density, proj_values, block_index, live_points):
    band = lax.axis_index("band")
    weights = occupation.astype(f32) * 0.001
    far_pairs = [(0, 2), (2, 0), (1, 3), (3, 1)]

    point_ids = lax.broadcasted_iota(i32, block_index.shape, 1)
    beta = proj_values * (point_ids < live_points[:, None]).astype(f32)[:, None, :]
    x = block_index >> 18
    y = (block_index >> 9) & 511
    c = (block_index >> 7) & 3
    lanes = block_index & 127
    from_rows = ((x * 64 + (y >> 3)) * 4 + c) * 16 + (y & 7)
    own = (y - 128 * band) & 511
    pair = (x & 1) * 2
    inside = jnp.where(
        own < 128,
        (x & 1) * 128 + own,
        jnp.where(own >= 510, LOW + pair + own - 510, HIGH + pair + own - 128),
    )
    into_rows = jnp.where(
        (own < 130) | (own >= 510), ((x >> 1) * 4 + c) * GROUP + inside, ACC_ROWS
    )

    strengths, outer_sum, near, far = front(
        weights, from_rows, lanes, beta, core_density, orbitals
    )
    far = lax.ppermute(far, "band", far_pairs)
    d0, d3, aug = scatter(into_rows, lanes, beta, strengths, outer_sum)
    above = lax.ppermute(d0, "dom", [((i + 1) % 32, i) for i in range(32)])
    below = lax.ppermute(d3, "dom", [(i, (i + 1) % 32) for i in range(32)])
    part, low, high = inner(d0, d3, near, far, aug)
    return outer(below, d0, d3, above, part, low, high)


def solution(mesh):
    placed = (
        P("band", "dom", None, None),
        P("band"),
        P("dom", "band", None),
        P("dom", None, None),
        P("dom", None),
        P("dom"),
    )
    return jax.shard_map(
        shards, mesh=mesh, in_specs=placed, out_specs=P("dom", "band", None), check_vma=False
    )
```

```python
import functools
import math

import jax
import jax.numpy as jnp
from jax import lax
from jax.experimental import pallas as pl
from jax.experimental.pallas import tpu as pltpu
from jax.sharding import PartitionSpec as P

f32 = jnp.float32
bf16 = jnp.bfloat16
i32 = jnp.int32

coef_a = 0.75 * (3.0 / math.pi) ** (1.0 / 3.0)
kappa_val = 0.804
mu_val = 0.2195149727645171
s_scale = 4.0 * (3.0 * math.pi**2) ** (2.0 / 3.0)
LOG2E = math.log2(math.e)

MIB = 2**20
GROUP = 264
LOW = 256
HIGH = 260
ACC_ROWS = 16 * GROUP
N_ACC = 8
NT = (((1,), (1,)), ((), ()))
VM = pl.BlockSpec(memory_space=pltpu.VMEM)
SM = pl.BlockSpec(memory_space=pltpu.SMEM)
ANY = pl.BlockSpec(memory_space=pl.ANY)
HBM = pl.BlockSpec(memory_space=pltpu.HBM)


def params(mib):
    return pltpu.CompilerParams(vmem_limit_bytes=mib * MIB)


MESH = pl.DeviceIdType.MESH
STEP = 8
ORDER = (0, 3, 1, 2)


def front_kernel(
    occupation, live, index, proj, core, orb,
    d0_ref, d3_ref, mid_ref,
    buf, picked, keep, send, recv, come, w_mine, w_core, w_come, rows_v, rows, beta, tile_of, row_of, vt,
    rows_sem, load_sem, swap_out, swap_in, far_out, far_in, w_out, w_in,
):
    band = lax.axis_index("band")
    dom = lax.axis_index("dom")
    parity = lax.rem(band, 2)
    z_hi = band // 2
    mate = (band + 1 - 2 * parity, dom)
    opposite = (lax.rem(band + 2, 4), dom)

    def loads(gi):
        made = []
        for i in range(2):
            x = 2 * ORDER[gi] + i
            for o in range(2):
                made.append(
                    pltpu.make_async_copy(
                        orb.at[o, x], buf.at[pl.ds(256 * x, 256), o], load_sem.at[4 * gi + 2 * i + o]
                    )
                )
        return made

    for gi in range(2):
        for copy in loads(gi):
            copy.start()
    barrier = pltpu.get_barrier_semaphore()
    for partner in (mate, opposite):
        pl.semaphore_signal(barrier, inc=1, device_id=partner, device_id_type=MESH)
    w0 = occupation[0].astype(f32) * 0.001
    w1 = occupation[1].astype(f32) * 0.001

    cell = index[...]
    x = cell >> 18
    y = (cell >> 9) & 511
    c = (cell >> 7) & 3
    rows_v[...] = ((x * 64 + (y >> 3)) * 4 + c) * 16 + (y & 7)
    to_rows = pltpu.make_async_copy(rows_v, rows, rows_sem.at[0])
    to_rows.start()
    own = (y - 128 * band) & 511
    g = x >> 1
    tile = jnp.where(g == 0, 0, jnp.where(g == 3, 1, g + 1)) * 4 + c
    pair = (x & 1) * 2
    rim = tile * 8 + pair + jnp.where(own >= 510, own - 510, own - 124)
    is_rim = (own >= 510) | (own < 130)
    tile_of[...] = jnp.where(own < 128, tile, jnp.where(is_rim, 16, -1))
    row_of[...] = jnp.where(own < 128, (x & 1) * 128 + own, rim).astype(f32)

    def squares(tile, count):
        a = buf[pl.ds(tile, count), 0]
        b = buf[pl.ds(tile, count), 1]
        return w0 * a * a + w1 * b * b

    def fill(ref, gi, near, mine):
        q = 2 * (z_hi if near else 1 - z_hi) + (parity if mine else 1 - parity)
        for i in range(2):
            x = 2 * ORDER[gi] + i

            def body(j, _):
                value = squares(x * 256 + q * 64 + 16 * j, 16)
                if near and mine:
                    value = value + core[x, pl.ds(16 * j, 16)]
                ref[near, gi, pl.ds(16 * i + 4 * j, 4)] = value.reshape(4, 4, 8, 128)
                return 0

            lax.fori_loop(0, 4, body, 0)
            q_low = lax.rem(q + 3, 4)
            own = jnp.where(q_low == band, 1.0, 0.0)
            value = squares(x * 256 + q_low * 64 + 60, 4) + own * core[x, 60:64]
            ref[near, gi, 32, :, 2 * i : 2 * i + 2, :] = value[:, 6:8, :]
            q_high = lax.rem(q + 1, 4)
            own = jnp.where(q_high == band, 1.0, 0.0)
            value = squares(x * 256 + q_high * 64, 4) + own * core[x, 0:4]
            ref[near, gi, 32, :, 4 + 2 * i : 6 + 2 * i, :] = value[:, 0:2, :]

    def swap(near, gi):
        return pltpu.make_async_remote_copy(
            src_ref=send.at[near, gi],
            dst_ref=recv.at[near, gi],
            send_sem=swap_out.at[4 * near + gi],
            recv_sem=swap_in.at[4 * near + gi],
            device_id=mate,
            device_id_type=MESH,
        )

    def across(gi, half):
        part = pl.ds(0, 16) if half == 0 else pl.ds(16, 17)
        return pltpu.make_async_remote_copy(
            src_ref=keep.at[0, gi, part],
            dst_ref=come.at[gi, part],
            send_sem=far_out.at[2 * gi + half],
            recv_sem=far_in.at[2 * gi + half],
            device_id=opposite,
            device_id_type=MESH,
        )

    def add_received(near, gi):
        def body(j, _):
            here = pl.ds(3 * j, 3)
            keep[near, gi, here] = keep[near, gi, here] + recv[near, gi, here]
            return 0

        lax.fori_loop(0, 11, body, 0)

    for gi in range(4):
        for copy in loads(gi):
            copy.wait()
        if gi < 2:
            for copy in loads(gi + 2):
                copy.start()
        fill(send, gi, 0, False)
        if gi == 0:
            pl.semaphore_wait(barrier, 2)
        swap(0, gi).start()
        fill(keep, gi, 0, True)
        fill(send, gi, 1, False)
        swap(1, gi).start()
        fill(keep, gi, 1, True)
        swap(0, gi).wait()
        add_received(0, gi)
        if gi < 2:
            across(gi, 0).start()
        if gi < 1:
            across(gi, 1).start()

    flat = buf.reshape(32768, 128)
    sub = lax.broadcasted_iota(i32, (128, 128), 0)
    two = lax.broadcasted_iota(i32, (256, 128), 0) - 2 * lax.broadcasted_iota(i32, (256, 128), 1)
    even = two == 0
    odd = two == 1
    lane_ids = lax.broadcasted_iota(i32, (8, 128), 1)
    to_rows.wait()

    def gather_step(i, total):
        for j in range(STEP):
            for k in range(128):
                r = rows[STEP * i + j, k]
                picked[pl.ds(256 * j + 2 * k, 2), :] = flat[pl.ds(r, 2, stride=8), :]
        for j in range(STEP):
            b = STEP * i + j
            hot = jnp.where((index[pl.ds(b, 1), :] & 127) == sub, 1.0, 0.0).astype(bf16)
            g = picked[256 * j : 256 * j + 256]
            g1 = g.astype(bf16)
            g2 = (g - g1.astype(f32)).astype(bf16)
            t = jnp.dot(g1, hot, preferred_element_type=f32) + jnp.dot(g2, hot, preferred_element_type=f32)
            be = jnp.where(lane_ids < live[b], proj[b], 0.0)
            beta[b] = be
            p0 = jnp.sum(jnp.where(even, t, 0.0), axis=0, keepdims=True)
            p1 = jnp.sum(jnp.where(odd, t, 0.0), axis=0, keepdims=True)
            c0 = jnp.sum(be * p0, axis=1, keepdims=True)
            c1 = jnp.sum(be * p1, axis=1, keepdims=True)
            total = jnp.where(lane_ids == b, w0 * c0 * c0 + w1 * c1 * c1, total)
        return total

    w_mine[...] = lax.fori_loop(0, 64 // STEP, gather_step, jnp.zeros((8, 128), f32))

    def send_w(src, at, target):
        return pltpu.make_async_remote_copy(
            src_ref=src,
            dst_ref=w_come.at[at],
            send_sem=w_out.at[at],
            recv_sem=w_in.at[at],
            device_id=target,
            device_id_type=MESH,
        )

    first = send_w(w_mine, 0, mate)
    first.start()
    for gi in range(2):
        swap(1, gi).wait()
        add_received(1, gi)
    first.wait()
    w_core[...] = w_mine[...] + w_come[0]
    second = send_w(w_core, 1, opposite)
    second.start()
    across(1, 1).start()
    for gi in range(2, 4):
        for half in range(2):
            across(gi, half).start()
    for gi in range(2, 4):
        swap(1, gi).wait()
        add_received(1, gi)
    second.wait()
    strengths = w_core[...] + w_come[1]

    def spread_step(b, _):
        be = beta[b]
        w = jnp.sum(jnp.where(lane_ids == b, strengths, 0.0), axis=1, keepdims=True)
        at = jnp.sum(w * be * be, axis=0, keepdims=True)
        a1 = at.astype(bf16).astype(f32)
        hot = (index[pl.ds(b, 1), :] & 127) == sub
        here = pl.ds(pl.multiple_of(128 * b, 128), 128)
        vt[0:128, here] = jnp.where(hot, a1, 0.0).astype(bf16)
        vt[128:256, here] = jnp.where(hot, at - a1, 0.0).astype(bf16)
        return 0

    lax.fori_loop(0, 64, spread_step, 0)

    def spread_tile(t, count):
        ids = lax.broadcasted_iota(i32, (count, 128), 0).astype(f32).astype(bf16)
        acc = jnp.zeros((count, 256), f32)
        for q in range(8):
            hots = []
            for b in range(8 * q, 8 * q + 8):
                at = jnp.where(tile_of[b : b + 1, :] == t, row_of[b : b + 1, :], -1.0).astype(bf16)
                hots.append(jnp.where(at == ids, jnp.ones((), bf16), jnp.zeros((), bf16)))
            acc = acc + lax.dot_general(
                jnp.concatenate(hots, axis=1),
                vt[:, 1024 * q : 1024 * q + 1024],
                NT,
                preferred_element_type=f32,
            )
        return acc[:, :128] + acc[:, 128:]

    rim_rows = spread_tile(16, 128)
    picked[0:128, :] = rim_rows
    for gi in range(4):
        across(gi, 0).wait()
        across(gi, 1).wait()
        out = d0_ref if gi == 0 else d3_ref if gi == 1 else mid_ref.at[gi - 2]

        def columns(c, _):
            cols = pl.ds(pl.multiple_of(128 * c, 128), 128)
            sums = keep[1, gi, pl.ds(0, 33), c] + come[gi, pl.ds(0, 33), c]
            out[0:256, cols] = spread_tile(4 * gi + c, 256) + sums[0:32].reshape(256, 128)
            rim = picked[pl.ds(pl.multiple_of((4 * gi + c) * 8, 8), 8), :]
            out[256:264, cols] = rim + sums[32]
            return 0

        lax.fori_loop(0, 4, columns, 0)


def front(occupation, live, index, proj, core, orbitals):
    tiles = orbitals.reshape(2, 8, 64, 8, 4, 128).transpose(0, 1, 2, 4, 3, 5).reshape(2, 8, 256, 8, 128)
    core = core.reshape(8, 16, 8, 4, 128).transpose(0, 1, 3, 2, 4).reshape(8, 64, 8, 128)
    group = jax.ShapeDtypeStruct((GROUP, 512), f32)
    both = pltpu.VMEM((2, 4, 33, 4, 8, 128), f32)
    strengths = pltpu.VMEM((8, 128), f32)
    points = pltpu.VMEM((64, 128), i32)
    dma = pltpu.SemaphoreType.DMA
    return pl.pallas_call(
        front_kernel,
        in_specs=[SM, SM, VM, VM, VM, HBM],
        out_specs=[VM] * 3,
        out_shape=[group, group, jax.ShapeDtypeStruct((2, GROUP, 512), f32)],
        scratch_shapes=[
            pltpu.VMEM((2048, 2, 8, 128), f32),
            pltpu.VMEM((256 * STEP, 128), f32),
            both,
            both,
            both,
            pltpu.VMEM((4, 33, 4, 8, 128), f32),
            strengths,
            strengths,
            pltpu.VMEM((2, 8, 128), f32),
            points,
            pltpu.SMEM((64, 128), i32),
            pltpu.VMEM((64, 8, 128), f32),
            points,
            pltpu.VMEM((64, 128), f32),
            pltpu.VMEM((256, 8192), bf16),
            dma((1,)),
            dma((16,)),
            dma((8,)),
            dma((8,)),
            dma((8,)),
            dma((8,)),
            dma((2,)),
            dma((2,)),
        ],
        compiler_params=pltpu.CompilerParams(
            vmem_limit_bytes=60 * MIB, collective_id=0, has_side_effects=True
        ),
        cost_estimate=pl.CostEstimate(flops=100 * MIB, bytes_accessed=40 * MIB, transcendentals=0),
        name="front",
    )(occupation, live, index, proj, core, tiles)


def place_group(dens, plane, group, lead=None):
    for i in range(2):
        dens[plane + i, 16:144, :] = group[pl.ds(128 * i, 128), :]
        dens[plane + i, 14:16, :] = group[pl.ds(LOW + 2 * i, 2), :]
        dens[plane + i, 144:146, :] = group[pl.ds(HIGH + 2 * i, 2), :]


def local_parts(dens, x, row, count):
    mid = dens[x, pl.ds(row, count), :]
    gy = (dens[x, pl.ds(row + 1, count), :] - dens[x, pl.ds(row - 1, count), :]) * 0.5
    gx = (dens[x + 1, pl.ds(row, count), :] - dens[x - 1, pl.ds(row, count), :]) * 0.5
    gz = (pltpu.roll(mid, 511, 1) - pltpu.roll(mid, 1, 1)) * 0.5
    sigma = gy * gy + gx * gx + gz * gz
    logs = jnp.log(mid)
    cube = jnp.exp2(logs * (LOG2E / 3.0))
    inv_four = jnp.exp2(logs * (-4.0 * LOG2E / 3.0))
    reduced = sigma * (inv_four * inv_four) * (1.0 / s_scale)
    under = 1.0 + (mu_val / kappa_val) * reduced
    inv = pl.reciprocal(under, approx=True)
    inv = inv * (2.0 - under * inv)
    slope = mu_val * inv * inv
    factor = (1.0 + kappa_val) - kappa_val * inv
    e_n = (-4.0 / 3.0 * coef_a) * cube * (factor - 2.0 * reduced * slope)
    twice = (-2.0 * coef_a / s_scale) * inv_four * slope
    return e_n, twice * gy, twice * gx, twice * gz


STRIP = 16


def full_plane(dens, x, flux_y, put):
    for row in (8, 144):
        flux_y[pl.ds(row, 8), :] = local_parts(dens, x, row, 8)[1]
    for row in range(16, 144, STRIP):
        e_n, fy, fx, fz = local_parts(dens, x, row, STRIP)
        flux_y[pl.ds(row, STRIP), :] = fy
        put(row - 16, e_n - (pltpu.roll(fz, 511, 1) - pltpu.roll(fz, 1, 1)) * 0.5, fx)


def minus_y(flux_y, row):
    up = flux_y[pl.ds(row + 17, STRIP), :]
    down = flux_y[pl.ds(row + 15, STRIP), :]
    return (up - down) * 0.5


def inner_kernel(d0, d3, mid, pot_ref, low_ref, high_ref, dens, flux_x, flux_y):
    place_group(dens, 0, d0)
    place_group(dens, 6, d3)
    place_group(dens, 2, mid.at[0])
    place_group(dens, 4, mid.at[1])

    def plane(x, _):
        def put(row, value, fx):
            pot_ref[x, pl.ds(row, STRIP), :] = value
            flux_x[x, pl.ds(row, STRIP), :] = fx

        full_plane(dens, x, flux_y, put)
        for row in range(0, 128, STRIP):
            here = pl.ds(row, STRIP)
            pot_ref[x, here, :] = pot_ref[x, here, :] - minus_y(flux_y, row)
        return 0

    lax.fori_loop(1, 7, plane, 0)

    def across(x, _):
        for row in range(0, 128, STRIP):
            here = pl.ds(row, STRIP)
            pot_ref[x, here, :] = (
                pot_ref[x, here, :] - (flux_x[x + 1, here, :] - flux_x[x - 1, here, :]) * 0.5
            )
        return 0

    lax.fori_loop(2, 6, across, 0)
    pot_ref[1] = pot_ref[1] - flux_x[2] * 0.5
    pot_ref[6] = pot_ref[6] + flux_x[5] * 0.5
    pot_ref[0] = jnp.zeros((128, 512), f32)
    pot_ref[7] = jnp.zeros((128, 512), f32)
    low_ref[...] = flux_x[1]
    high_ref[...] = flux_x[6]


def inner(d0, d3, mid):
    whole2 = lambda *shape: pl.BlockSpec(shape, lambda s: (0,) * len(shape))
    plane = jax.ShapeDtypeStruct((128, 512), f32)
    return pl.pallas_call(
        inner_kernel,
        grid=(1,),
        in_specs=[whole2(GROUP, 512)] * 2 + [whole2(2, GROUP, 512)],
        out_specs=[whole2(8, 128, 512), whole2(128, 512), whole2(128, 512)],
        out_shape=[jax.ShapeDtypeStruct((8, 128, 512), f32), plane, plane],
        scratch_shapes=[
            pltpu.VMEM((8, 160, 512), f32),
            pltpu.VMEM((8, 128, 512), f32),
            pltpu.VMEM((160, 512), f32),
        ],
        compiler_params=params(60),
        cost_estimate=pl.CostEstimate(flops=100 * MIB, bytes_accessed=30 * MIB, transcendentals=0),
        name="inner_planes",
    )(d0, d3, mid)


def outer_kernel(below, d0, d3, above, old, low, high, pot_ref, dens, flux_x, flux_y):
    place_group(dens, 0, below)
    place_group(dens, 2, d0)
    place_group(dens, 4, d3)
    place_group(dens, 6, above)
    for row in range(0, 128, STRIP):
        flux_x[0, pl.ds(row, STRIP), :] = local_parts(dens, 1, row + 16, STRIP)[2]
        flux_x[1, pl.ds(row, STRIP), :] = local_parts(dens, 6, row + 16, STRIP)[2]

    for end, x, edge, inside in ((0, 2, 0, 1), (1, 5, 3, 2)):

        def put(row, value, fx):
            here = pl.ds(row, STRIP)
            pot_ref[edge, here, :] = value
            if end == 0:
                pot_ref[inside, here, :] = old[1, here, :] + 0.5 * fx
            else:
                pot_ref[inside, here, :] = old[2, here, :] - 0.5 * fx

        full_plane(dens, x, flux_y, put)
        for row in range(0, 128, STRIP):
            here = pl.ds(row, STRIP)
            if end == 0:
                across = (low[here, :] - flux_x[0, here, :]) * 0.5
            else:
                across = (flux_x[1, here, :] - high[here, :]) * 0.5
            pot_ref[edge, here, :] = pot_ref[edge, here, :] - minus_y(flux_y, row) - across


def outer_body(below, d0, d3, above, old_ref, low, high, pot_ref, dens, flux_x, flux_y, old, new, sem):
    ins = [
        pltpu.make_async_copy(old_ref.at[pl.ds(0, 2)], old.at[pl.ds(0, 2)], sem.at[0]),
        pltpu.make_async_copy(old_ref.at[pl.ds(6, 2)], old.at[pl.ds(2, 2)], sem.at[1]),
    ]
    for copy in ins:
        copy.start()
    for copy in ins:
        copy.wait()
    outer_kernel(below, d0, d3, above, old, low, high, new, dens, flux_x, flux_y)
    outs = [
        pltpu.make_async_copy(new.at[pl.ds(0, 2)], pot_ref.at[pl.ds(0, 2)], sem.at[2]),
        pltpu.make_async_copy(new.at[pl.ds(2, 2)], pot_ref.at[pl.ds(6, 2)], sem.at[3]),
    ]
    for copy in outs:
        copy.start()
    for copy in outs:
        copy.wait()


def outer(below, d0, d3, above, old, low, high):
    return pl.pallas_call(
        outer_body,
        in_specs=[VM, VM, VM, VM, ANY, VM, VM],
        out_specs=ANY,
        out_shape=jax.ShapeDtypeStruct((8, 128, 512), f32),
        input_output_aliases={4: 0},
        scratch_shapes=[
            pltpu.VMEM((8, 160, 512), f32),
            pltpu.VMEM((2, 128, 512), f32),
            pltpu.VMEM((160, 512), f32),
            pltpu.VMEM((4, 128, 512), f32),
            pltpu.VMEM((4, 128, 512), f32),
            pltpu.SemaphoreType.DMA((4,)),
        ],
        compiler_params=params(60),
        cost_estimate=pl.CostEstimate(flops=100 * MIB, bytes_accessed=30 * MIB, transcendentals=0),
        name="outer_planes",
    )(below, d0, d3, above, old, low, high)


def shards(orbitals, occupation, core_density, proj_values, block_index, live_points):
    d0, d3, mid = front(
        occupation, live_points, block_index, proj_values, core_density, orbitals
    )
    above = lax.ppermute(d0, "dom", [((i + 1) % 32, i) for i in range(32)])
    below = lax.ppermute(d3, "dom", [(i, (i + 1) % 32) for i in range(32)])
    part, low, high = inner(d0, d3, mid)
    return outer(below, d0, d3, above, part, low, high)


def solution(mesh):
    placed = (
        P("band", "dom", None, None),
        P("band"),
        P("dom", "band", None),
        P("dom", None, None),
        P("dom", None),
        P("dom"),
    )
    return jax.shard_map(
        shards, mesh=mesh, in_specs=placed, out_specs=P("dom", "band", None), check_vma=False
    )
```

```python
import functools
import math

import jax
import jax.numpy as jnp
from jax import lax
from jax.experimental import pallas as pl
from jax.experimental.pallas import tpu as pltpu
from jax.sharding import PartitionSpec as P

f32 = jnp.float32
bf16 = jnp.bfloat16
i32 = jnp.int32

coef_a = 0.75 * (3.0 / math.pi) ** (1.0 / 3.0)
kappa_val = 0.804
mu_val = 0.2195149727645171
s_scale = 4.0 * (3.0 * math.pi**2) ** (2.0 / 3.0)
LOG2E = math.log2(math.e)

MIB = 2**20
GROUP = 264
LOW = 256
HIGH = 260
ACC_ROWS = 16 * GROUP
N_ACC = 8
NT = (((1,), (1,)), ((), ()))
VM = pl.BlockSpec(memory_space=pltpu.VMEM)
SM = pl.BlockSpec(memory_space=pltpu.SMEM)
ANY = pl.BlockSpec(memory_space=pl.ANY)
HBM = pl.BlockSpec(memory_space=pltpu.HBM)


def params(mib):
    return pltpu.CompilerParams(vmem_limit_bytes=mib * MIB)


def local_parts(dens, x, row, count):
    mid = dens[x, pl.ds(row, count), :]
    gy = (dens[x, pl.ds(row + 1, count), :] - dens[x, pl.ds(row - 1, count), :]) * 0.5
    gx = (dens[x + 1, pl.ds(row, count), :] - dens[x - 1, pl.ds(row, count), :]) * 0.5
    gz = (pltpu.roll(mid, 511, 1) - pltpu.roll(mid, 1, 1)) * 0.5
    sigma = gy * gy + gx * gx + gz * gz
    logs = jnp.log(mid)
    cube = jnp.exp2(logs * (LOG2E / 3.0))
    inv_four = jnp.exp2(logs * (-4.0 * LOG2E / 3.0))
    reduced = sigma * (inv_four * inv_four) * (1.0 / s_scale)
    under = 1.0 + (mu_val / kappa_val) * reduced
    inv = pl.reciprocal(under, approx=True)
    inv = inv * (2.0 - under * inv)
    slope = mu_val * inv * inv
    factor = (1.0 + kappa_val) - kappa_val * inv
    e_n = (-4.0 / 3.0 * coef_a) * cube * (factor - 2.0 * reduced * slope)
    twice = (-2.0 * coef_a / s_scale) * inv_four * slope
    return e_n, twice * gy, twice * gx, twice * gz


STRIP = 16


def full_plane(dens, x, flux_y, put):
    for row in (8, 144):
        flux_y[pl.ds(row, 8), :] = local_parts(dens, x, row, 8)[1]
    for row in range(16, 144, STRIP):
        e_n, fy, fx, fz = local_parts(dens, x, row, STRIP)
        flux_y[pl.ds(row, STRIP), :] = fy
        put(row - 16, e_n - (pltpu.roll(fz, 511, 1) - pltpu.roll(fz, 1, 1)) * 0.5, fx)


def minus_y(flux_y, row):
    up = flux_y[pl.ds(row + 17, STRIP), :]
    down = flux_y[pl.ds(row + 15, STRIP), :]
    return (up - down) * 0.5


MESH = pl.DeviceIdType.MESH
STEP = 8
ORDER = (0, 3, 1, 2)


def potential_kernel(
    occupation, live, index, proj, core, orb,
    pot_ref,
    buf, picked_a, picked_b, rims, dens, flux_x, flux_y, keep, send, recv, come, w_mine, w_core, w_come, rows_v, rows, beta, tile_of, row_of, vt,
    rows_sem, load_sem, swap_out, swap_in, far_out, far_in, w_out, w_in, halo_out, halo_in,
):
    band = lax.axis_index("band")
    dom = lax.axis_index("dom")
    parity = lax.rem(band, 2)
    z_hi = band // 2
    mate = (band + 1 - 2 * parity, dom)
    opposite = (lax.rem(band + 2, 4), dom)
    after = (band, lax.rem(dom + 1, 32))
    before = (band, lax.rem(dom + 31, 32))

    def loads(gi):
        made = []
        for i in range(2):
            x = 2 * ORDER[gi] + i
            for o in range(2):
                made.append(
                    pltpu.make_async_copy(
                        orb.at[o, x], buf.at[pl.ds(256 * x, 256), o], load_sem.at[4 * gi + 2 * i + o]
                    )
                )
        return made

    for gi in range(2):
        for copy in loads(gi):
            copy.start()
    barrier = pltpu.get_barrier_semaphore()
    for partner in (mate, opposite, after, before):
        pl.semaphore_signal(barrier, inc=1, device_id=partner, device_id_type=MESH)
    w0 = occupation[0].astype(f32) * 0.001
    w1 = occupation[1].astype(f32) * 0.001

    cell = index[...]
    x = cell >> 18
    y = (cell >> 9) & 511
    c = (cell >> 7) & 3
    rows_v[...] = ((x * 64 + (y >> 3)) * 4 + c) * 16 + (y & 7)
    to_rows = pltpu.make_async_copy(rows_v, rows, rows_sem.at[0])
    to_rows.start()
    own = (y - 128 * band) & 511
    g = x >> 1
    tile = jnp.where(g == 0, 0, jnp.where(g == 3, 1, g + 1)) * 4 + c
    pair = (x & 1) * 2
    rim = tile * 8 + pair + jnp.where(own >= 510, own - 510, own - 124)
    is_rim = (own >= 510) | (own < 130)
    tile_of[...] = jnp.where(own < 128, tile, jnp.where(is_rim, 16, -1))
    row_of[...] = jnp.where(own < 128, (x & 1) * 128 + own, rim).astype(f32)

    def squares(tile, count):
        a = buf[pl.ds(tile, count), 0]
        b = buf[pl.ds(tile, count), 1]
        return w0 * a * a + w1 * b * b

    def fill(ref, gi, near, mine):
        q = 2 * (z_hi if near else 1 - z_hi) + (parity if mine else 1 - parity)
        for i in range(2):
            x = 2 * ORDER[gi] + i

            def body(j, _):
                value = squares(x * 256 + q * 64 + 16 * j, 16)
                if near and mine:
                    value = value + core[x, pl.ds(16 * j, 16)]
                ref[near, gi, pl.ds(16 * i + 4 * j, 4)] = value.reshape(4, 4, 8, 128)
                return 0

            lax.fori_loop(0, 4, body, 0, unroll=2)
            q_low = lax.rem(q + 3, 4)
            own = jnp.where(q_low == band, 1.0, 0.0)
            value = squares(x * 256 + q_low * 64 + 60, 4) + own * core[x, 60:64]
            ref[near, gi, 32, :, 2 * i : 2 * i + 2, :] = value[:, 6:8, :]
            q_high = lax.rem(q + 1, 4)
            own = jnp.where(q_high == band, 1.0, 0.0)
            value = squares(x * 256 + q_high * 64, 4) + own * core[x, 0:4]
            ref[near, gi, 32, :, 4 + 2 * i : 6 + 2 * i, :] = value[:, 0:2, :]

    def swap(near, gi):
        return pltpu.make_async_remote_copy(
            src_ref=send.at[near, gi],
            dst_ref=recv.at[near, gi],
            send_sem=swap_out.at[4 * near + gi],
            recv_sem=swap_in.at[4 * near + gi],
            device_id=mate,
            device_id_type=MESH,
        )

    def across(gi, half):
        part = pl.ds(0, 16) if half == 0 else pl.ds(16, 17)
        return pltpu.make_async_remote_copy(
            src_ref=keep.at[0, gi, part],
            dst_ref=come.at[gi, part],
            send_sem=far_out.at[2 * gi + half],
            recv_sem=far_in.at[2 * gi + half],
            device_id=opposite,
            device_id_type=MESH,
        )

    def add_received(near, gi):
        def body(j, _):
            here = pl.ds(3 * j, 3)
            keep[near, gi, here] = keep[near, gi, here] + recv[near, gi, here]
            return 0

        lax.fori_loop(0, 11, body, 0)

    for gi in range(4):
        for copy in loads(gi):
            copy.wait()
        if gi < 2:
            for copy in loads(gi + 2):
                copy.start()
        fill(send, gi, 0, False)
        if gi == 0:
            pl.semaphore_wait(barrier, 4)
        swap(0, gi).start()
        fill(keep, gi, 0, True)
        fill(send, gi, 1, False)
        swap(1, gi).start()
        fill(keep, gi, 1, True)
        swap(0, gi).wait()
        add_received(0, gi)
        if gi < 2:
            across(gi, 0).start()
        if gi < 1:
            across(gi, 1).start()

    flat = buf.reshape(32768, 128)
    sub = lax.broadcasted_iota(i32, (128, 128), 0)
    two = lax.broadcasted_iota(i32, (256, 128), 0) - 2 * lax.broadcasted_iota(i32, (256, 128), 1)
    even = two == 0
    odd = two == 1
    lane_ids = lax.broadcasted_iota(i32, (8, 128), 1)
    to_rows.wait()

    def pick(step, j, picked):
        for k in range(128):
            r = rows[STEP * step + j, k]
            picked[pl.ds(256 * j + 2 * k, 2), :] = flat[pl.ds(r, 2, stride=8), :]

    def project(step, j, picked, total):
        b = STEP * step + j
        hot = jnp.where((index[pl.ds(b, 1), :] & 127) == sub, 1.0, 0.0).astype(bf16)
        g = picked[256 * j : 256 * j + 256]
        g1 = g.astype(bf16)
        g2 = (g - g1.astype(f32)).astype(bf16)
        t = jnp.dot(g1, hot, preferred_element_type=f32) + jnp.dot(g2, hot, preferred_element_type=f32)
        be = jnp.where(lane_ids < live[b], proj[b], 0.0)
        beta[b] = be
        p0 = jnp.sum(jnp.where(even, t, 0.0), axis=0, keepdims=True)
        p1 = jnp.sum(jnp.where(odd, t, 0.0), axis=0, keepdims=True)
        c0 = jnp.sum(be * p0, axis=1, keepdims=True)
        c1 = jnp.sum(be * p1, axis=1, keepdims=True)
        return jnp.where(lane_ids == b, w0 * c0 * c0 + w1 * c1 * c1, total)

    def gather_step(i, total):
        for j in range(STEP):
            pick(2 * i + 1, j, picked_b)
            total = project(2 * i, j, picked_a, total)
        for j in range(STEP):
            pick(jnp.minimum(2 * i + 2, 64 // STEP - 1), j, picked_a)
            total = project(2 * i + 1, j, picked_b, total)
        return total

    for j in range(STEP):
        pick(0, j, picked_a)
    w_mine[...] = lax.fori_loop(0, 32 // STEP, gather_step, jnp.zeros((8, 128), f32))

    def send_w(src, at, target):
        return pltpu.make_async_remote_copy(
            src_ref=src,
            dst_ref=w_come.at[at],
            send_sem=w_out.at[at],
            recv_sem=w_in.at[at],
            device_id=target,
            device_id_type=MESH,
        )

    first = send_w(w_mine, 0, mate)
    first.start()
    for gi in range(2):
        swap(1, gi).wait()
        add_received(1, gi)
    first.wait()
    w_core[...] = w_mine[...] + w_come[0]
    second = send_w(w_core, 1, opposite)
    second.start()
    across(1, 1).start()
    for gi in range(2, 4):
        for half in range(2):
            across(gi, half).start()
    for gi in range(2, 4):
        swap(1, gi).wait()
        add_received(1, gi)
    second.wait()
    strengths = w_core[...] + w_come[1]

    def spread_step(i, _):
        for j in range(STEP):
            b = STEP * i + j
            be = beta[b]
            w = jnp.sum(jnp.where(lane_ids == b, strengths, 0.0), axis=1, keepdims=True)
            at = jnp.sum(w * be * be, axis=0, keepdims=True)
            a1 = at.astype(bf16).astype(f32)
            hot = (index[pl.ds(b, 1), :] & 127) == sub
            here = pl.ds(pl.multiple_of(128 * STEP * i, 128 * STEP) + 128 * j, 128)
            vt[0:128, here] = jnp.where(hot, a1, 0.0).astype(bf16)
            vt[128:256, here] = jnp.where(hot, at - a1, 0.0).astype(bf16)
        return 0

    lax.fori_loop(0, 64 // STEP, spread_step, 0)

    def spread_tile(t, count):
        ids = lax.broadcasted_iota(i32, (count, 128), 0).astype(f32).astype(bf16)
        acc = jnp.zeros((count, 256), f32)
        for q in range(8):
            hots = []
            for b in range(8 * q, 8 * q + 8):
                at = jnp.where(tile_of[b : b + 1, :] == t, row_of[b : b + 1, :], -1.0).astype(bf16)
                hots.append(jnp.where(at == ids, jnp.ones((), bf16), jnp.zeros((), bf16)))
            acc = acc + lax.dot_general(
                jnp.concatenate(hots, axis=1),
                vt[:, 1024 * q : 1024 * q + 1024],
                NT,
                preferred_element_type=f32,
            )
        return acc[:, :128] + acc[:, 128:]

    rims[...] = spread_tile(16, 128)

    def density(gi, arrived):
        at = 2 + 2 * ORDER[gi]

        def columns(c, _):
            cols = pl.ds(pl.multiple_of(128 * c, 128), 128)
            sums = keep[1, gi, pl.ds(0, 33), c]
            if arrived:
                sums = sums + come[gi, pl.ds(0, 33), c]
            body = spread_tile(4 * gi + c, 256) + sums[0:32].reshape(256, 128)
            rim = rims[pl.ds(pl.multiple_of((4 * gi + c) * 8, 8), 8), :] + sums[32]
            for i in range(2):
                dens[at + i, 16:144, cols] = body[128 * i : 128 * i + 128]
                dens[at + i, 14:16, cols] = rim[2 * i : 2 * i + 2]
                dens[at + i, 144:146, cols] = rim[4 + 2 * i : 6 + 2 * i]
            return 0

        lax.fori_loop(0, 4, columns, 0)

    def add_arrived(gi):
        at = 2 + 2 * ORDER[gi]

        def columns(c, _):
            cols = pl.ds(pl.multiple_of(128 * c, 128), 128)
            rim = come[gi, 32, c]
            for i in range(2):
                dens[at + i, 16:144, cols] = dens[at + i, 16:144, cols] + come[
                    gi, pl.ds(16 * i, 16), c
                ].reshape(128, 128)
                dens[at + i, 14:16, cols] = dens[at + i, 14:16, cols] + rim[2 * i : 2 * i + 2]
                dens[at + i, 144:146, cols] = dens[at + i, 144:146, cols] + rim[4 + 2 * i : 6 + 2 * i]
            return 0

        lax.fori_loop(0, 4, columns, 0)

    def halo(at, source, target, row, count, partner):
        return pltpu.make_async_remote_copy(
            src_ref=dens.at[source, pl.ds(row, count)],
            dst_ref=dens.at[target, pl.ds(row, count)],
            send_sem=halo_out.at[at],
            recv_sem=halo_in.at[at],
            device_id=partner,
            device_id_type=MESH,
        )

    def wait_far(gi):
        across(gi, 0).wait()
        across(gi, 1).wait()

    def plane(x, _):
        def put(row, value, fx):
            pot_ref[x, pl.ds(row, STRIP), :] = value
            flux_x[x + 1, pl.ds(row, STRIP), :] = fx

        full_plane(dens, x + 2, flux_y, put)
        for row in range(0, 128, STRIP):
            here = pl.ds(row, STRIP)
            pot_ref[x, here, :] = pot_ref[x, here, :] - minus_y(flux_y, row)
        return 0

    def along_x(x, _):
        for row in range(0, 128, STRIP):
            here = pl.ds(row, STRIP)
            pot_ref[x, here, :] = (
                pot_ref[x, here, :] - (flux_x[x + 2, here, :] - flux_x[x, here, :]) * 0.5
            )
        return 0

    wait_far(0)
    density(0, True)
    halos = [halo(0, 2, 10, 8, 144, before), halo(1, 3, 11, 16, 128, before)]
    for copy in halos:
        copy.start()
    wait_far(1)
    density(1, True)
    more = [halo(2, 9, 1, 8, 144, after), halo(3, 8, 0, 16, 128, after)]
    for copy in more:
        copy.start()
    wait_far(2)
    density(2, True)
    lax.fori_loop(1, 3, plane, 0)
    density(3, False)
    wait_far(3)
    add_arrived(3)
    lax.fori_loop(3, 7, plane, 0)
    lax.fori_loop(2, 6, along_x, 0)
    for copy in halos + more:
        copy.wait()

    def rest(e, _):
        at = 9 * e
        for row in range(0, 128, STRIP):
            flux_x[at, pl.ds(row, STRIP), :] = local_parts(dens, at + 1, row + 16, STRIP)[2]
        plane(7 * e, 0)
        along_x(6 * e, 0)
        along_x(6 * e + 1, 0)
        return 0

    lax.fori_loop(0, 2, rest, 0)


def potential(occupation, live, index, proj, core, orbitals):
    tiles = orbitals.reshape(2, 8, 64, 8, 4, 128).transpose(0, 1, 2, 4, 3, 5).reshape(2, 8, 256, 8, 128)
    core = core.reshape(8, 16, 8, 4, 128).transpose(0, 1, 3, 2, 4).reshape(8, 64, 8, 128)
    both = pltpu.VMEM((2, 4, 33, 4, 8, 128), f32)
    strengths = pltpu.VMEM((8, 128), f32)
    points = pltpu.VMEM((64, 128), i32)
    dma = pltpu.SemaphoreType.DMA
    return pl.pallas_call(
        potential_kernel,
        in_specs=[SM, SM, VM, VM, VM, HBM],
        out_specs=VM,
        out_shape=jax.ShapeDtypeStruct((8, 128, 512), f32),
        scratch_shapes=[
            pltpu.VMEM((2048, 2, 8, 128), f32),
            pltpu.VMEM((256 * STEP, 128), f32),
            pltpu.VMEM((256 * STEP, 128), f32),
            pltpu.VMEM((128, 128), f32),
            pltpu.VMEM((12, 160, 512), f32),
            pltpu.VMEM((10, 128, 512), f32),
            pltpu.VMEM((160, 512), f32),
            both,
            both,
            both,
            pltpu.VMEM((4, 33, 4, 8, 128), f32),
            strengths,
            strengths,
            pltpu.VMEM((2, 8, 128), f32),
            points,
            pltpu.SMEM((64, 128), i32),
            pltpu.VMEM((64, 8, 128), f32),
            points,
            pltpu.VMEM((64, 128), f32),
            pltpu.VMEM((256, 8192), bf16),
            dma((1,)),
            dma((16,)),
            dma((8,)),
            dma((8,)),
            dma((8,)),
            dma((8,)),
            dma((2,)),
            dma((2,)),
            dma((4,)),
            dma((4,)),
        ],
        compiler_params=pltpu.CompilerParams(
            vmem_limit_bytes=60 * MIB, collective_id=0, has_side_effects=True
        ),
        cost_estimate=pl.CostEstimate(flops=100 * MIB, bytes_accessed=40 * MIB, transcendentals=0),
        name="potential",
    )(occupation, live, index, proj, core, tiles)


def shards(orbitals, occupation, core_density, proj_values, block_index, live_points):
    return potential(
        occupation, live_points, block_index, proj_values, core_density, orbitals
    )


def solution(mesh):
    placed = (
        P("band", "dom", None, None),
        P("band"),
        P("dom", "band", None),
        P("dom", None, None),
        P("dom", None),
        P("dom"),
    )
    return jax.shard_map(
        shards, mesh=mesh, in_specs=placed, out_specs=P("dom", "band", None), check_vma=False
    )
```

```python
import functools
import math

import jax
import jax.numpy as jnp
from jax import lax
from jax.experimental import pallas as pl
from jax.experimental.pallas import tpu as pltpu
from jax.sharding import PartitionSpec as P

f32 = jnp.float32
bf16 = jnp.bfloat16
i32 = jnp.int32

coef_a = 0.75 * (3.0 / math.pi) ** (1.0 / 3.0)
kappa_val = 0.804
mu_val = 0.2195149727645171
s_scale = 4.0 * (3.0 * math.pi**2) ** (2.0 / 3.0)
LOG2E = math.log2(math.e)

MIB = 2**20
GROUP = 264
LOW = 256
HIGH = 260
ACC_ROWS = 16 * GROUP
N_ACC = 8
NT = (((1,), (1,)), ((), ()))
VM = pl.BlockSpec(memory_space=pltpu.VMEM)
SM = pl.BlockSpec(memory_space=pltpu.SMEM)
ANY = pl.BlockSpec(memory_space=pl.ANY)
HBM = pl.BlockSpec(memory_space=pltpu.HBM)


def params(mib):
    return pltpu.CompilerParams(vmem_limit_bytes=mib * MIB)


def local_parts(dens, x, row, count):
    mid = dens[x, pl.ds(row, count), :]
    gy = (dens[x, pl.ds(row + 1, count), :] - dens[x, pl.ds(row - 1, count), :]) * 0.5
    gx = (dens[x + 1, pl.ds(row, count), :] - dens[x - 1, pl.ds(row, count), :]) * 0.5
    gz = (pltpu.roll(mid, 511, 1) - pltpu.roll(mid, 1, 1)) * 0.5
    sigma = gy * gy + gx * gx + gz * gz
    logs = jnp.log(mid)
    cube = jnp.exp2(logs * (LOG2E / 3.0))
    inv_four = jnp.exp2(logs * (-4.0 * LOG2E / 3.0))
    reduced = sigma * (inv_four * inv_four) * (1.0 / s_scale)
    under = 1.0 + (mu_val / kappa_val) * reduced
    inv = pl.reciprocal(under, approx=True)
    inv = inv * (2.0 - under * inv)
    slope = mu_val * inv * inv
    factor = (1.0 + kappa_val) - kappa_val * inv
    e_n = (-4.0 / 3.0 * coef_a) * cube * (factor - 2.0 * reduced * slope)
    twice = (-2.0 * coef_a / s_scale) * inv_four * slope
    return e_n, twice * gy, twice * gx, twice * gz


STRIP = 16


def full_plane(dens, x, flux_y, put):
    for row in (8, 144):
        flux_y[pl.ds(row, 8), :] = local_parts(dens, x, row, 8)[1]
    for row in range(16, 144, STRIP):
        e_n, fy, fx, fz = local_parts(dens, x, row, STRIP)
        flux_y[pl.ds(row, STRIP), :] = fy
        put(row - 16, e_n - (pltpu.roll(fz, 511, 1) - pltpu.roll(fz, 1, 1)) * 0.5, fx)


def minus_y(flux_y, row):
    up = flux_y[pl.ds(row + 17, STRIP), :]
    down = flux_y[pl.ds(row + 15, STRIP), :]
    return (up - down) * 0.5


MESH = pl.DeviceIdType.MESH
STEP = 8
ORDER = (0, 3, 1, 2)


def potential_kernel(
    occupation, live, index, proj, core, orb,
    pot_ref,
    buf, picked_a, picked_b, rims, dens, flux_x, flux_y, keep, send, recv, come, w_mine, w_core, w_come, rows_v, rows, beta, tile_of, row_of, vt,
    rows_sem, load_sem, swap_out, swap_in, far_out, far_in, w_out, w_in, halo_out, halo_in,
    hop1, hop2, hop1_out, hop1_in, hop2_out, hop2_in, hop3_out, hop3_in, rim_out, rim_in,
):
    band = lax.axis_index("band")
    dom = lax.axis_index("dom")
    parity = lax.rem(band, 2)
    z_hi = band // 2
    mate = (band + 1 - 2 * parity, dom)
    opposite = (lax.rem(band + 2, 4), dom)
    after = (band, lax.rem(dom + 1, 32))
    before = (band, lax.rem(dom + 31, 32))

    def loads(gi):
        made = []
        for i in range(2):
            x = 2 * ORDER[gi] + i
            for o in range(2):
                made.append(
                    pltpu.make_async_copy(
                        orb.at[o, x], buf.at[pl.ds(256 * x, 256), o], load_sem.at[4 * gi + 2 * i + o]
                    )
                )
        return made

    for gi in range(2):
        for copy in loads(gi):
            copy.start()
    barrier = pltpu.get_barrier_semaphore()
    spot = lax.rem(dom, 16)
    layer = dom - spot
    in_last = spot >= 12
    in_row = in_last | (spot < 4)
    lane = jnp.where(in_last, spot - 12, spot)
    row_first = jnp.where(in_last, layer + 12, layer)
    sender = jnp.where(in_last, layer, layer + 15)
    taker = jnp.where(in_last, layer + 15, layer)
    far_first = jnp.where(in_last, layer, layer + 12)
    is_last = spot == 15
    is_first = spot == 0
    is_end = is_last | is_first
    other_layer = (band, lax.rem(dom + 16, 32))

    def greet(partner):
        pl.semaphore_signal(barrier, inc=1, device_id=partner, device_id_type=MESH)

    for partner in (mate, opposite, after, before):
        greet(partner)

    @pl.when(in_row)
    def _():
        greet(other_layer)
        greet((band, sender))

    @pl.when(in_row & jnp.logical_not(is_end))
    def _():
        greet((band, taker))

    @pl.when(is_end)
    def _():
        for k in range(4):
            greet((band, far_first + k))

            @pl.when(lane != k)
            def _():
                greet((band, row_first + k))

    w0 = occupation[0].astype(f32) * 0.001
    w1 = occupation[1].astype(f32) * 0.001

    cell = index[...]
    x = cell >> 18
    y = (cell >> 9) & 511
    c = (cell >> 7) & 3
    rows_v[...] = ((x * 64 + (y >> 3)) * 4 + c) * 16 + (y & 7)
    to_rows = pltpu.make_async_copy(rows_v, rows, rows_sem.at[0])
    to_rows.start()
    own = (y - 128 * band) & 511
    g = x >> 1
    tile = jnp.where(g == 0, 0, jnp.where(g == 3, 1, g + 1)) * 4 + c
    pair = (x & 1) * 2
    rim = tile * 8 + pair + jnp.where(own >= 510, own - 510, own - 124)
    is_rim = (own >= 510) | (own < 130)
    tile_of[...] = jnp.where(own < 128, tile, jnp.where(is_rim, 16, -1))
    row_of[...] = jnp.where(own < 128, (x & 1) * 128 + own, rim).astype(f32)

    def squares(tile, count):
        a = buf[pl.ds(tile, count), 0]
        b = buf[pl.ds(tile, count), 1]
        return w0 * a * a + w1 * b * b

    def fill(ref, gi, near, mine):
        q = 2 * (z_hi if near else 1 - z_hi) + (parity if mine else 1 - parity)
        for i in range(2):
            x = 2 * ORDER[gi] + i

            def body(j, _):
                value = squares(x * 256 + q * 64 + 16 * j, 16)
                if near and mine:
                    value = value + core[x, pl.ds(16 * j, 16)]
                ref[near, gi, pl.ds(16 * i + 4 * j, 4)] = value.reshape(4, 4, 8, 128)
                return 0

            lax.fori_loop(0, 4, body, 0, unroll=2)
            q_low = lax.rem(q + 3, 4)
            own = jnp.where(q_low == band, 1.0, 0.0)
            value = squares(x * 256 + q_low * 64 + 60, 4) + own * core[x, 60:64]
            ref[near, gi, 32, :, 2 * i : 2 * i + 2, :] = value[:, 6:8, :]
            q_high = lax.rem(q + 1, 4)
            own = jnp.where(q_high == band, 1.0, 0.0)
            value = squares(x * 256 + q_high * 64, 4) + own * core[x, 0:4]
            ref[near, gi, 32, :, 4 + 2 * i : 6 + 2 * i, :] = value[:, 0:2, :]

    def swap(near, gi):
        return pltpu.make_async_remote_copy(
            src_ref=send.at[near, gi],
            dst_ref=recv.at[near, gi],
            send_sem=swap_out.at[4 * near + gi],
            recv_sem=swap_in.at[4 * near + gi],
            device_id=mate,
            device_id_type=MESH,
        )

    def across(gi, half):
        part = pl.ds(0, 16) if half == 0 else pl.ds(16, 17)
        return pltpu.make_async_remote_copy(
            src_ref=keep.at[0, gi, part],
            dst_ref=come.at[gi, part],
            send_sem=far_out.at[2 * gi + half],
            recv_sem=far_in.at[2 * gi + half],
            device_id=opposite,
            device_id_type=MESH,
        )

    def add_received(near, gi):
        def body(j, _):
            here = pl.ds(3 * j, 3)
            keep[near, gi, here] = keep[near, gi, here] + recv[near, gi, here]
            return 0

        lax.fori_loop(0, 11, body, 0)

    for gi in range(4):
        for copy in loads(gi):
            copy.wait()
        if gi < 2:
            for copy in loads(gi + 2):
                copy.start()
        fill(send, gi, 0, False)
        if gi == 0:
            pl.semaphore_wait(barrier, jnp.where(is_end, 13, jnp.where(in_row, 7, 4)))
        swap(0, gi).start()
        fill(keep, gi, 0, True)
        fill(send, gi, 1, False)
        swap(1, gi).start()
        fill(keep, gi, 1, True)
        swap(0, gi).wait()
        add_received(0, gi)
        if gi < 2:
            across(gi, 0).start()
        if gi < 1:
            across(gi, 1).start()

    flat = buf.reshape(32768, 128)
    sub = lax.broadcasted_iota(i32, (128, 128), 0)
    two = lax.broadcasted_iota(i32, (256, 128), 0) - 2 * lax.broadcasted_iota(i32, (256, 128), 1)
    even = two == 0
    odd = two == 1
    lane_ids = lax.broadcasted_iota(i32, (8, 128), 1)
    to_rows.wait()

    def pick(step, j, picked):
        for k in range(128):
            r = rows[STEP * step + j, k]
            picked[pl.ds(256 * j + 2 * k, 2), :] = flat[pl.ds(r, 2, stride=8), :]

    def project(step, j, picked, total):
        b = STEP * step + j
        hot = jnp.where((index[pl.ds(b, 1), :] & 127) == sub, 1.0, 0.0).astype(bf16)
        g = picked[256 * j : 256 * j + 256]
        g1 = g.astype(bf16)
        g2 = (g - g1.astype(f32)).astype(bf16)
        t = jnp.dot(g1, hot, preferred_element_type=f32) + jnp.dot(g2, hot, preferred_element_type=f32)
        be = jnp.where(lane_ids < live[b], proj[b], 0.0)
        beta[b] = be
        p0 = jnp.sum(jnp.where(even, t, 0.0), axis=0, keepdims=True)
        p1 = jnp.sum(jnp.where(odd, t, 0.0), axis=0, keepdims=True)
        c0 = jnp.sum(be * p0, axis=1, keepdims=True)
        c1 = jnp.sum(be * p1, axis=1, keepdims=True)
        return jnp.where(lane_ids == b, w0 * c0 * c0 + w1 * c1 * c1, total)

    def gather_step(i, total):
        for j in range(STEP):
            pick(2 * i + 1, j, picked_b)
            total = project(2 * i, j, picked_a, total)
        for j in range(STEP):
            pick(jnp.minimum(2 * i + 2, 64 // STEP - 1), j, picked_a)
            total = project(2 * i + 1, j, picked_b, total)
        return total

    for j in range(STEP):
        pick(0, j, picked_a)
    w_mine[...] = lax.fori_loop(0, 32 // STEP, gather_step, jnp.zeros((8, 128), f32))

    def send_w(src, at, target):
        return pltpu.make_async_remote_copy(
            src_ref=src,
            dst_ref=w_come.at[at],
            send_sem=w_out.at[at],
            recv_sem=w_in.at[at],
            device_id=target,
            device_id_type=MESH,
        )

    first = send_w(w_mine, 0, mate)
    first.start()
    for gi in range(2):
        swap(1, gi).wait()
        add_received(1, gi)
    first.wait()
    w_core[...] = w_mine[...] + w_come[0]
    second = send_w(w_core, 1, opposite)
    second.start()
    across(1, 1).start()
    across(2, 0).start()
    for gi in range(2, 4):
        swap(1, gi).wait()
        add_received(1, gi)
    second.wait()
    strengths = w_core[...] + w_come[1]

    def spread_step(i, _):
        for j in range(STEP):
            b = STEP * i + j
            be = beta[b]
            w = jnp.sum(jnp.where(lane_ids == b, strengths, 0.0), axis=1, keepdims=True)
            at = jnp.sum(w * be * be, axis=0, keepdims=True)
            a1 = at.astype(bf16).astype(f32)
            hot = (index[pl.ds(b, 1), :] & 127) == sub
            here = pl.ds(pl.multiple_of(128 * STEP * i, 128 * STEP) + 128 * j, 128)
            vt[0:128, here] = jnp.where(hot, a1, 0.0).astype(bf16)
            vt[128:256, here] = jnp.where(hot, at - a1, 0.0).astype(bf16)
        return 0

    lax.fori_loop(0, 64 // STEP, spread_step, 0)

    def spread_tile(t, count):
        ids = lax.broadcasted_iota(i32, (count, 128), 0).astype(f32).astype(bf16)
        acc = jnp.zeros((count, 256), f32)
        for q in range(8):
            hots = []
            for b in range(8 * q, 8 * q + 8):
                at = jnp.where(tile_of[b : b + 1, :] == t, row_of[b : b + 1, :], -1.0).astype(bf16)
                hots.append(jnp.where(at == ids, jnp.ones((), bf16), jnp.zeros((), bf16)))
            acc = acc + lax.dot_general(
                jnp.concatenate(hots, axis=1),
                vt[:, 1024 * q : 1024 * q + 1024],
                NT,
                preferred_element_type=f32,
            )
        return acc[:, :128] + acc[:, 128:]

    rims[...] = spread_tile(16, 128)

    def density(gi, arrived):
        at = 2 + 2 * ORDER[gi]

        def columns(c, _):
            cols = pl.ds(pl.multiple_of(128 * c, 128), 128)
            sums = keep[1, gi, pl.ds(0, 33), c]
            if arrived:
                sums = sums + come[gi, pl.ds(0, 33), c]
            body = spread_tile(4 * gi + c, 256) + sums[0:32].reshape(256, 128)
            rim = rims[pl.ds(pl.multiple_of((4 * gi + c) * 8, 8), 8), :] + sums[32]
            for i in range(2):
                dens[at + i, 16:144, cols] = body[128 * i : 128 * i + 128]
                dens[at + i, 14:16, cols] = rim[2 * i : 2 * i + 2]
                dens[at + i, 144:146, cols] = rim[4 + 2 * i : 6 + 2 * i]
            return 0

        lax.fori_loop(0, 4, columns, 0)

    def add_arrived(gi):
        at = 2 + 2 * ORDER[gi]

        def columns(c, _):
            cols = pl.ds(pl.multiple_of(128 * c, 128), 128)
            rim = come[gi, 32, c]
            for i in range(2):
                dens[at + i, 16:144, cols] = dens[at + i, 16:144, cols] + come[
                    gi, pl.ds(16 * i, 16), c
                ].reshape(128, 128)
                dens[at + i, 14:16, cols] = dens[at + i, 14:16, cols] + rim[2 * i : 2 * i + 2]
                dens[at + i, 144:146, cols] = dens[at + i, 144:146, cols] + rim[4 + 2 * i : 6 + 2 * i]
            return 0

        lax.fori_loop(0, 4, columns, 0)

    def halo(at, source, target, row, count, partner):
        return pltpu.make_async_remote_copy(
            src_ref=dens.at[source, pl.ds(row, count)],
            dst_ref=dens.at[target, pl.ds(row, count)],
            send_sem=halo_out.at[at],
            recv_sem=halo_in.at[at],
            device_id=partner,
            device_id_type=MESH,
        )

    def wait_far(gi):
        across(gi, 0).wait()
        across(gi, 1).wait()

    def plane(x, _):
        def put(row, value, fx):
            pot_ref[x, pl.ds(row, STRIP), :] = value
            flux_x[x + 1, pl.ds(row, STRIP), :] = fx

        full_plane(dens, x + 2, flux_y, put)
        for row in range(0, 128, STRIP):
            here = pl.ds(row, STRIP)
            pot_ref[x, here, :] = pot_ref[x, here, :] - minus_y(flux_y, row)
        return 0

    def along_x(x, _):
        for row in range(0, 128, STRIP):
            here = pl.ds(row, STRIP)
            pot_ref[x, here, :] = (
                pot_ref[x, here, :] - (flux_x[x + 2, here, :] - flux_x[x, here, :]) * 0.5
            )
        return 0

    def remote(src, dst, out, came, partner):
        return pltpu.make_async_remote_copy(
            src_ref=src,
            dst_ref=dst,
            send_sem=out,
            recv_sem=came,
            device_id=partner,
            device_id_type=MESH,
        )

    def part(plane, k):
        return dens.at[pl.ds(plane, 2), pl.ds(pl.multiple_of(16 + 32 * k, 8), 32)]

    gives = jnp.where(in_last, 8, 2)
    lands = jnp.where(in_last, 10, 0)

    def to_row(k):
        return remote(part(gives, k), hop1, hop1_out.at[k], hop1_in.at[0], (band, far_first + k))

    def across_to_row():
        return remote(hop1, hop2, hop2_out.at[0], hop2_in.at[0], other_layer)

    def across_to_taker():
        return remote(hop1, part(lands, lane), hop2_out.at[0], hop3_in.at[lane], other_layer)

    def to_taker():
        return remote(hop2, part(lands, lane), hop3_out.at[0], hop3_in.at[lane], (band, taker))

    def from_row(k):
        return remote(hop2, part(lands, k), hop3_out.at[0], hop3_in.at[k], (band, taker))

    def rim_copy(j):
        here = pl.ds(8 + 136 * j, 8)
        return remote(
            dens.at[jnp.where(in_last, 9, 2), here],
            dens.at[jnp.where(in_last, 1, 10), here],
            rim_out.at[j],
            rim_in.at[j],
            (band, lax.rem(dom + jnp.where(in_last, 1, 31), 32)),
        )

    def send_by_parts():
        for k in range(4):
            to_row(k).start()
        for j in range(2):
            rim_copy(j).start()

    def start(copies):
        for copy in copies:
            copy.start()

    def arrived(copies):
        for copy in copies:
            copy.wait_recv()

    to_before = [halo(0, 2, 10, 8, 144, before), halo(1, 3, 11, 16, 128, before)]
    to_after = [halo(2, 9, 1, 8, 144, after), halo(3, 8, 0, 16, 128, after)]
    wait_far(0)
    density(0, True)
    across(2, 1).start()
    pl.when(is_first)(send_by_parts)
    pl.when(jnp.logical_not(is_first))(lambda: start(to_before))
    wait_far(1)
    density(1, True)
    across(3, 0).start()
    pl.when(is_last)(send_by_parts)
    pl.when(jnp.logical_not(is_last))(lambda: start(to_after))
    wait_far(2)
    density(2, True)

    across(3, 1).start()
    lax.fori_loop(1, 3, plane, 0)
    density(3, False)

    @pl.when(in_row)
    def _():
        to_row(0).wait_recv()

        @pl.when(is_end)
        def _():
            across_to_taker().start()

        @pl.when(jnp.logical_not(is_end))
        def _():
            across_to_row().start()

    wait_far(3)
    add_arrived(3)
    lax.fori_loop(3, 5, plane, 0)

    @pl.when(in_row & jnp.logical_not(is_end))
    def _():
        across_to_row().wait_recv()
        to_taker().start()

    lax.fori_loop(5, 7, plane, 0)
    lax.fori_loop(2, 6, along_x, 0)

    def rest(e):
        at = 9 * e
        for row in range(0, 128, STRIP):
            flux_x[at, pl.ds(row, STRIP), :] = local_parts(dens, at + 1, row + 16, STRIP)[2]
        plane(7 * e, 0)
        along_x(6 * e, 0)
        along_x(6 * e + 1, 0)

    def by_parts():
        for j in range(2):
            rim_copy(j).wait_recv()
        for k in range(4):
            from_row(k).wait_recv()

    pl.when(is_first)(lambda: arrived(to_before))
    pl.when(jnp.logical_not(is_first))(lambda: arrived(to_after))
    rest(jnp.where(is_first, 1, 0))
    pl.when(is_end)(by_parts)
    pl.when(jnp.logical_not(is_end))(lambda: arrived(to_before))
    rest(jnp.where(is_first, 0, 1))

    @pl.when(jnp.logical_not(is_first))
    def _():
        for copy in to_before:
            copy.wait_send()

    @pl.when(jnp.logical_not(is_last))
    def _():
        for copy in to_after:
            copy.wait_send()

    @pl.when(in_row)
    def _():
        across_to_row().wait_send()

    @pl.when(in_row & jnp.logical_not(is_end))
    def _():
        to_taker().wait_send()

    @pl.when(is_end)
    def _():
        for j in range(2):
            rim_copy(j).wait_send()
        for k in range(4):
            to_row(k).wait_send()


def potential(occupation, live, index, proj, core, orbitals):
    tiles = orbitals.reshape(2, 8, 64, 8, 4, 128).transpose(0, 1, 2, 4, 3, 5).reshape(2, 8, 256, 8, 128)
    core = core.reshape(8, 16, 8, 4, 128).transpose(0, 1, 3, 2, 4).reshape(8, 64, 8, 128)
    both = pltpu.VMEM((2, 4, 33, 4, 8, 128), f32)
    strengths = pltpu.VMEM((8, 128), f32)
    points = pltpu.VMEM((64, 128), i32)
    dma = pltpu.SemaphoreType.DMA
    return pl.pallas_call(
        potential_kernel,
        in_specs=[SM, SM, VM, VM, VM, HBM],
        out_specs=VM,
        out_shape=jax.ShapeDtypeStruct((8, 128, 512), f32),
        scratch_shapes=[
            pltpu.VMEM((2048, 2, 8, 128), f32),
            pltpu.VMEM((256 * STEP, 128), f32),
            pltpu.VMEM((256 * STEP, 128), f32),
            pltpu.VMEM((128, 128), f32),
            pltpu.VMEM((12, 160, 512), f32),
            pltpu.VMEM((10, 128, 512), f32),
            pltpu.VMEM((160, 512), f32),
            both,
            both,
            both,
            pltpu.VMEM((4, 33, 4, 8, 128), f32),
            strengths,
            strengths,
            pltpu.VMEM((2, 8, 128), f32),
            points,
            pltpu.SMEM((64, 128), i32),
            pltpu.VMEM((64, 8, 128), f32),
            points,
            pltpu.VMEM((64, 128), f32),
            pltpu.VMEM((256, 8192), bf16),
            dma((1,)),
            dma((16,)),
            dma((8,)),
            dma((8,)),
            dma((8,)),
            dma((8,)),
            dma((2,)),
            dma((2,)),
            dma((4,)),
            dma((4,)),
            pltpu.VMEM((2, 32, 512), f32),
            pltpu.VMEM((2, 32, 512), f32),
            dma((4,)),
            dma((1,)),
            dma((1,)),
            dma((1,)),
            dma((1,)),
            dma((4,)),
            dma((2,)),
            dma((2,)),
        ],
        compiler_params=pltpu.CompilerParams(
            vmem_limit_bytes=60 * MIB, collective_id=0, has_side_effects=True
        ),
        cost_estimate=pl.CostEstimate(flops=100 * MIB, bytes_accessed=40 * MIB, transcendentals=0),
        name="potential",
    )(occupation, live, index, proj, core, tiles)


def shards(orbitals, occupation, core_density, proj_values, block_index, live_points):
    return potential(
        occupation, live_points, block_index, proj_values, core_density, orbitals
    )


def solution(mesh):
    placed = (
        P("band", "dom", None, None),
        P("band"),
        P("dom", "band", None),
        P("dom", None, None),
        P("dom", None),
        P("dom"),
    )
    return jax.shard_map(
        shards, mesh=mesh, in_specs=placed, out_specs=P("dom", "band", None), check_vma=False
    )
```

```python
import functools
import math

import jax
import jax.numpy as jnp
from jax import lax
from jax.experimental import pallas as pl
from jax.experimental.pallas import tpu as pltpu
from jax.sharding import PartitionSpec as P

f32 = jnp.float32
bf16 = jnp.bfloat16
i32 = jnp.int32

coef_a = 0.75 * (3.0 / math.pi) ** (1.0 / 3.0)
kappa_val = 0.804
mu_val = 0.2195149727645171
s_scale = 4.0 * (3.0 * math.pi**2) ** (2.0 / 3.0)
LOG2E = math.log2(math.e)

MIB = 2**20
GROUP = 264
LOW = 256
HIGH = 260
ACC_ROWS = 16 * GROUP
N_ACC = 8
NT = (((1,), (1,)), ((), ()))
VM = pl.BlockSpec(memory_space=pltpu.VMEM)
SM = pl.BlockSpec(memory_space=pltpu.SMEM)
ANY = pl.BlockSpec(memory_space=pl.ANY)
HBM = pl.BlockSpec(memory_space=pltpu.HBM)


def params(mib):
    return pltpu.CompilerParams(vmem_limit_bytes=mib * MIB)


def local_parts(dens, x, row, count):
    mid = dens[x, pl.ds(row, count), :]
    gy = (dens[x, pl.ds(row + 1, count), :] - dens[x, pl.ds(row - 1, count), :]) * 0.5
    gx = (dens[x + 1, pl.ds(row, count), :] - dens[x - 1, pl.ds(row, count), :]) * 0.5
    gz = (pltpu.roll(mid, 511, 1) - pltpu.roll(mid, 1, 1)) * 0.5
    sigma = gy * gy + gx * gx + gz * gz
    logs = jnp.log(mid)
    cube = jnp.exp2(logs * (LOG2E / 3.0))
    inv_four = jnp.exp2(logs * (-4.0 * LOG2E / 3.0))
    reduced = sigma * (inv_four * inv_four) * (1.0 / s_scale)
    under = 1.0 + (mu_val / kappa_val) * reduced
    inv = pl.reciprocal(under, approx=True)
    inv = inv * (2.0 - under * inv)
    slope = mu_val * inv * inv
    factor = (1.0 + kappa_val) - kappa_val * inv
    e_n = (-4.0 / 3.0 * coef_a) * cube * (factor - 2.0 * reduced * slope)
    twice = (-2.0 * coef_a / s_scale) * inv_four * slope
    return e_n, twice * gy, twice * gx, twice * gz


STRIP = 32


def full_plane(dens, x, flux_y, put):
    for row in (8, 144):
        flux_y[pl.ds(row, 8), :] = local_parts(dens, x, row, 8)[1]
    for row in range(16, 144, STRIP):
        e_n, fy, fx, fz = local_parts(dens, x, row, STRIP)
        flux_y[pl.ds(row, STRIP), :] = fy
        put(row - 16, e_n - (pltpu.roll(fz, 511, 1) - pltpu.roll(fz, 1, 1)) * 0.5, fx)


def minus_y(flux_y, row):
    up = flux_y[pl.ds(row + 17, STRIP), :]
    down = flux_y[pl.ds(row + 15, STRIP), :]
    return (up - down) * 0.5


MESH = pl.DeviceIdType.MESH
STEP = 8
ORDER = (0, 3, 1, 2)


def potential_kernel(
    occupation, live, index, proj_hbm, core_hbm, orb,
    pot_ref,
    proj, core,
    buf, picked_a, picked_b, rims, dens, flux_x, flux_y, keep, send, recv, come, w_mine, w_core, w_come, rows_v, rows, beta, tile_of, row_of, vt,
    rows_sem, load_sem, swap_out, swap_in, far_out, far_in, w_out, w_in, halo_out, halo_in,
    hop1, hop2, hop1_out, hop1_in, hop2_out, hop2_in, hop3_out, hop3_in, rim_out, rim_in,
):
    band = lax.axis_index("band")
    dom = lax.axis_index("dom")
    parity = lax.rem(band, 2)
    z_hi = band // 2
    mate = (band + 1 - 2 * parity, dom)
    opposite = (lax.rem(band + 2, 4), dom)
    after = (band, lax.rem(dom + 1, 32))
    before = (band, lax.rem(dom + 31, 32))

    def loads(gi):
        made = []
        for i in range(2):
            x = 2 * ORDER[gi] + i
            for o in range(2):
                made.append(
                    pltpu.make_async_copy(
                        orb.at[o, x], buf.at[pl.ds(256 * x, 256), o], load_sem.at[4 * gi + 2 * i + o]
                    )
                )
        return made

    for copy in loads(0):
        copy.start()
    core_in = pltpu.make_async_copy(core_hbm, core, rows_sem.at[1])
    proj_in = pltpu.make_async_copy(proj_hbm, proj, rows_sem.at[2])
    core_in.start()
    proj_in.start()
    barrier = pltpu.get_barrier_semaphore()
    spot = lax.rem(dom, 16)
    layer = dom - spot
    in_last = spot >= 12
    lane = jnp.where(in_last, spot - 12, spot)
    in_row = (in_last & (lane != 1)) | ((spot < 4) & (lane != 2))
    row_first = jnp.where(in_last, layer + 12, layer)
    sender = jnp.where(in_last, layer, layer + 15)
    taker = jnp.where(in_last, layer + 15, layer)
    far_first = jnp.where(in_last, layer, layer + 12)
    is_last = spot == 15
    is_first = spot == 0
    is_end = is_last | is_first
    other_layer = (band, lax.rem(dom + 16, 32))

    def greet(partner):
        pl.semaphore_signal(barrier, inc=1, device_id=partner, device_id_type=MESH)

    for partner in (mate, opposite, after, before):
        greet(partner)

    @pl.when(in_row)
    def _():
        greet(other_layer)
        greet((band, sender))

    @pl.when(in_row & jnp.logical_not(is_end))
    def _():
        greet((band, taker))

    far_lanes = (jnp.where(in_last, 0, 3), jnp.where(in_last, 1, 2), jnp.where(in_last, 3, 0))
    near_lanes = (jnp.where(in_last, 2, 1), jnp.where(in_last, 0, 3))

    @pl.when(is_end)
    def _():
        for k in far_lanes:
            greet((band, far_first + k))
        for k in near_lanes:
            greet((band, row_first + k))

    w0 = occupation[0].astype(f32) * 0.001
    w1 = occupation[1].astype(f32) * 0.001

    cell = index[...]
    x = cell >> 18
    y = (cell >> 9) & 511
    c = (cell >> 7) & 3
    rows_v[...] = ((x * 64 + (y >> 3)) * 4 + c) * 16 + (y & 7)
    to_rows = pltpu.make_async_copy(rows_v, rows, rows_sem.at[0])
    to_rows.start()
    own = (y - 128 * band) & 511
    g = x >> 1
    tile = jnp.where(g == 0, 0, jnp.where(g == 3, 1, g + 1)) * 4 + c
    pair = (x & 1) * 2
    rim = tile * 8 + pair + jnp.where(own >= 510, own - 510, own - 124)
    is_rim = (own >= 510) | (own < 130)
    tile_of[...] = jnp.where(own < 128, tile, jnp.where(is_rim, 16, -1))
    row_of[...] = jnp.where(own < 128, (x & 1) * 128 + own, rim).astype(f32)

    def squares(tile, count):
        a = buf[pl.ds(tile, count), 0]
        b = buf[pl.ds(tile, count), 1]
        return w0 * a * a + w1 * b * b

    def fill(ref, gi, near, mine):
        q = 2 * (z_hi if near else 1 - z_hi) + (parity if mine else 1 - parity)
        for i in range(2):
            x = 2 * ORDER[gi] + i

            def body(j, _):
                value = squares(x * 256 + q * 64 + 16 * j, 16)
                if near and mine:
                    value = value + core[x, pl.ds(16 * j, 16)]
                ref[near, gi, pl.ds(16 * i + 4 * j, 4)] = value.reshape(4, 4, 8, 128)
                return 0

            lax.fori_loop(0, 4, body, 0, unroll=2)
            q_low = lax.rem(q + 3, 4)
            own = jnp.where(q_low == band, 1.0, 0.0)
            value = squares(x * 256 + q_low * 64 + 60, 4) + own * core[x, 60:64]
            ref[near, gi, 32, :, 2 * i : 2 * i + 2, :] = value[:, 6:8, :]
            q_high = lax.rem(q + 1, 4)
            own = jnp.where(q_high == band, 1.0, 0.0)
            value = squares(x * 256 + q_high * 64, 4) + own * core[x, 0:4]
            ref[near, gi, 32, :, 4 + 2 * i : 6 + 2 * i, :] = value[:, 0:2, :]

    def swap(near, gi):
        return pltpu.make_async_remote_copy(
            src_ref=send.at[near, gi],
            dst_ref=recv.at[near, gi],
            send_sem=swap_out.at[4 * near + gi],
            recv_sem=swap_in.at[4 * near + gi],
            device_id=mate,
            device_id_type=MESH,
        )

    def across(gi, half):
        part = pl.ds(0, 16) if half == 0 else pl.ds(16, 17)
        return pltpu.make_async_remote_copy(
            src_ref=keep.at[0, gi, part],
            dst_ref=come.at[gi, part],
            send_sem=far_out.at[2 * gi + half],
            recv_sem=far_in.at[2 * gi + half],
            device_id=opposite,
            device_id_type=MESH,
        )

    def add_received(near, gi):
        def body(j, _):
            here = pl.ds(3 * j, 3)
            keep[near, gi, here] = keep[near, gi, here] + recv[near, gi, here]
            return 0

        lax.fori_loop(0, 11, body, 0)

    for gi in range(4):
        for copy in loads(gi):
            copy.wait()
        if gi < 3:
            for copy in loads(gi + 1):
                copy.start()
        if gi == 0:
            core_in.wait()
        fill(send, gi, 0, False)
        if gi == 0:
            pl.semaphore_wait(barrier, jnp.where(is_end, 11, jnp.where(in_row, 7, 4)))
        swap(0, gi).start()
        fill(keep, gi, 0, True)
        fill(send, gi, 1, False)
        swap(1, gi).start()
        if gi > 0:
            fill(keep, gi, 1, True)
        swap(0, gi).wait()
        add_received(0, gi)
        if gi < 2:
            across(gi, 0).start()
        if gi < 1:
            across(gi, 1).start()
            fill(keep, gi, 1, True)

    proj_in.wait()
    flat = buf.reshape(32768, 128)
    sub = lax.broadcasted_iota(i32, (128, 128), 0)
    two = lax.broadcasted_iota(i32, (256, 128), 0) - 2 * lax.broadcasted_iota(i32, (256, 128), 1)
    even = two == 0
    odd = two == 1
    lane_ids = lax.broadcasted_iota(i32, (8, 128), 1)
    to_rows.wait()

    def pick(step, j, picked):
        for k in range(128):
            r = rows[STEP * step + j, k]
            picked[pl.ds(256 * j + 2 * k, 2), :] = flat[pl.ds(r, 2, stride=8), :]

    def project(step, j, picked, total):
        b = STEP * step + j
        hot = jnp.where((index[pl.ds(b, 1), :] & 127) == sub, 1.0, 0.0).astype(bf16)
        g = picked[256 * j : 256 * j + 256]
        g1 = g.astype(bf16)
        g2 = (g - g1.astype(f32)).astype(bf16)
        t = jnp.dot(g1, hot, preferred_element_type=f32) + jnp.dot(g2, hot, preferred_element_type=f32)
        be = jnp.where(lane_ids < live[b], proj[b], 0.0)
        beta[b] = be
        p0 = jnp.sum(jnp.where(even, t, 0.0), axis=0, keepdims=True)
        p1 = jnp.sum(jnp.where(odd, t, 0.0), axis=0, keepdims=True)
        c0 = jnp.sum(be * p0, axis=1, keepdims=True)
        c1 = jnp.sum(be * p1, axis=1, keepdims=True)
        return jnp.where(lane_ids == b, w0 * c0 * c0 + w1 * c1 * c1, total)

    def gather_step(i, total):
        for j in range(STEP):
            pick(2 * i + 1, j, picked_b)
            total = project(2 * i, j, picked_a, total)
        for j in range(STEP):
            pick(jnp.minimum(2 * i + 2, 64 // STEP - 1), j, picked_a)
            total = project(2 * i + 1, j, picked_b, total)
        return total

    for j in range(STEP):
        pick(0, j, picked_a)
    w_mine[...] = lax.fori_loop(0, 32 // STEP, gather_step, jnp.zeros((8, 128), f32))

    def send_w(src, at, target):
        return pltpu.make_async_remote_copy(
            src_ref=src,
            dst_ref=w_come.at[at],
            send_sem=w_out.at[at],
            recv_sem=w_in.at[at],
            device_id=target,
            device_id_type=MESH,
        )

    first = send_w(w_mine, 0, mate)
    first.start()
    for gi in range(2):
        swap(1, gi).wait()
        add_received(1, gi)
    first.wait()
    w_core[...] = w_mine[...] + w_come[0]
    second = send_w(w_core, 1, opposite)
    second.start()
    across(1, 1).start()
    across(2, 0).start()
    for gi in range(2, 4):
        swap(1, gi).wait()
        add_received(1, gi)
    second.wait()
    strengths = w_core[...] + w_come[1]

    def spread_step(i, _):
        for j in range(STEP):
            b = STEP * i + j
            be = beta[b]
            w = jnp.sum(jnp.where(lane_ids == b, strengths, 0.0), axis=1, keepdims=True)
            at = jnp.sum(w * be * be, axis=0, keepdims=True)
            a1 = at.astype(bf16).astype(f32)
            hot = (index[pl.ds(b, 1), :] & 127) == sub
            here = pl.ds(pl.multiple_of(128 * STEP * i, 128 * STEP) + 128 * j, 128)
            vt[0:128, here] = jnp.where(hot, a1, 0.0).astype(bf16)
            vt[128:256, here] = jnp.where(hot, at - a1, 0.0).astype(bf16)
        return 0

    lax.fori_loop(0, 64 // STEP, spread_step, 0)

    def spread_tiles(tiles, count):
        ids = lax.broadcasted_iota(i32, (count, 128), 0).astype(f32).astype(bf16)
        acc = jnp.zeros((count * len(tiles), 256), f32)
        for q in range(8):
            strips = []
            for t in tiles:
                hots = []
                for b in range(8 * q, 8 * q + 8):
                    at = jnp.where(tile_of[b : b + 1, :] == t, row_of[b : b + 1, :], -1.0).astype(bf16)
                    hots.append(jnp.where(at == ids, jnp.ones((), bf16), jnp.zeros((), bf16)))
                strips.append(jnp.concatenate(hots, axis=1))
            acc = acc + lax.dot_general(
                jnp.concatenate(strips, axis=0),
                vt[:, 1024 * q : 1024 * q + 1024],
                NT,
                preferred_element_type=f32,
            )
        return acc[:, :128] + acc[:, 128:]

    rims[...] = spread_tiles((16,), 128)

    def density(gi, arrived):
        at = 2 + 2 * ORDER[gi]

        def columns(half, _):
            both = spread_tiles((4 * gi + 2 * half, 4 * gi + 2 * half + 1), 256)
            for j in range(2):
                c = 2 * half + j
                cols = pl.ds(pl.multiple_of(128 * c, 128), 128)
                sums = keep[1, gi, pl.ds(0, 33), c]
                if arrived:
                    sums = sums + come[gi, pl.ds(0, 33), c]
                body = both[256 * j : 256 * j + 256] + sums[0:32].reshape(256, 128)
                rim = rims[pl.ds(pl.multiple_of((4 * gi + c) * 8, 8), 8), :] + sums[32]
                for i in range(2):
                    dens[at + i, 16:144, cols] = body[128 * i : 128 * i + 128]
                    dens[at + i, 14:16, cols] = rim[2 * i : 2 * i + 2]
                    dens[at + i, 144:146, cols] = rim[4 + 2 * i : 6 + 2 * i]
            return 0

        lax.fori_loop(0, 2, columns, 0)

    def add_arrived(gi):
        at = 2 + 2 * ORDER[gi]

        def columns(c, _):
            cols = pl.ds(pl.multiple_of(128 * c, 128), 128)
            rim = come[gi, 32, c]
            for i in range(2):
                dens[at + i, 16:144, cols] = dens[at + i, 16:144, cols] + come[
                    gi, pl.ds(16 * i, 16), c
                ].reshape(128, 128)
                dens[at + i, 14:16, cols] = dens[at + i, 14:16, cols] + rim[2 * i : 2 * i + 2]
                dens[at + i, 144:146, cols] = dens[at + i, 144:146, cols] + rim[4 + 2 * i : 6 + 2 * i]
            return 0

        lax.fori_loop(0, 4, columns, 0)

    def halo(at, source, target, row, count, partner):
        return pltpu.make_async_remote_copy(
            src_ref=dens.at[source, pl.ds(row, count)],
            dst_ref=dens.at[target, pl.ds(row, count)],
            send_sem=halo_out.at[at],
            recv_sem=halo_in.at[at],
            device_id=partner,
            device_id_type=MESH,
        )

    def wait_far(gi):
        across(gi, 0).wait()
        across(gi, 1).wait()

    def plane(x, _):
        def put(row, value, fx):
            pot_ref[x, pl.ds(row, STRIP), :] = value
            flux_x[x + 1, pl.ds(row, STRIP), :] = fx

        full_plane(dens, x + 2, flux_y, put)
        for row in range(0, 128, STRIP):
            here = pl.ds(row, STRIP)
            pot_ref[x, here, :] = pot_ref[x, here, :] - minus_y(flux_y, row)
        return 0

    def along_x(x, _):
        for row in range(0, 128, STRIP):
            here = pl.ds(row, STRIP)
            pot_ref[x, here, :] = (
                pot_ref[x, here, :] - (flux_x[x + 2, here, :] - flux_x[x, here, :]) * 0.5
            )
        return 0

    def remote(src, dst, out, came, partner):
        return pltpu.make_async_remote_copy(
            src_ref=src,
            dst_ref=dst,
            send_sem=out,
            recv_sem=came,
            device_id=partner,
            device_id_type=MESH,
        )

    def part(plane, k):
        return dens.at[pl.ds(plane, 2), pl.ds(pl.multiple_of(16 + 32 * k, 8), 32)]

    gives = jnp.where(in_last, 8, 2)
    lands = jnp.where(in_last, 10, 0)

    piece = jnp.where(in_last, jnp.where(lane == 2, 2, 3), jnp.where(lane == 1, 2, 3))

    def to_row(k):
        slot = k % 2 if k < 2 else 0
        target = (band, far_first + far_lanes[max(k - 1, 0)])
        return remote(part(gives, k), hop1.at[slot], hop1_out.at[k], hop1_in.at[slot], target)

    def across_to_row():
        return remote(hop1.at[0], hop2, hop2_out.at[0], hop2_in.at[0], other_layer)

    def across_to_taker(k):
        return remote(hop1.at[k], part(lands, k), hop2_out.at[k], hop3_in.at[k], other_layer)

    def to_taker():
        return remote(hop2, part(lands, piece), hop3_out.at[0], hop3_in.at[piece], (band, taker))

    def from_row(k):
        return remote(hop2, part(lands, k), hop3_out.at[0], hop3_in.at[k], (band, taker))

    def rim_copy(j):
        here = pl.ds(8 + 136 * j, 8)
        return remote(
            dens.at[jnp.where(in_last, 9, 2), here],
            dens.at[jnp.where(in_last, 1, 10), here],
            rim_out.at[j],
            rim_in.at[j],
            (band, lax.rem(dom + jnp.where(in_last, 1, 31), 32)),
        )

    def send_by_parts():
        for k in range(4):
            to_row(k).start()
        for j in range(2):
            rim_copy(j).start()

    def start(copies):
        for copy in copies:
            copy.start()

    def arrived(copies):
        for copy in copies:
            copy.wait_recv()

    to_before = [halo(0, 2, 10, 8, 144, before), halo(1, 3, 11, 16, 128, before)]
    to_after = [halo(2, 9, 1, 8, 144, after), halo(3, 8, 0, 16, 128, after)]
    wait_far(0)
    density(0, True)
    across(2, 1).start()
    pl.when(is_first)(send_by_parts)
    pl.when(jnp.logical_not(is_first))(lambda: start(to_before))
    wait_far(1)
    density(1, True)
    across(3, 0).start()
    pl.when(is_last)(send_by_parts)
    pl.when(jnp.logical_not(is_last))(lambda: start(to_after))
    wait_far(2)
    density(2, True)

    across(3, 1).start()
    lax.fori_loop(1, 3, plane, 0)
    density(3, False)

    @pl.when(is_end)
    def _():
        for k in range(2):
            to_row(k).wait_recv()
            across_to_taker(k).start()

    @pl.when(in_row & jnp.logical_not(is_end))
    def _():
        to_row(0).wait_recv()
        across_to_row().start()

    wait_far(3)
    add_arrived(3)
    lax.fori_loop(3, 5, plane, 0)

    @pl.when(in_row & jnp.logical_not(is_end))
    def _():
        across_to_row().wait_recv()
        to_taker().start()

    lax.fori_loop(5, 7, plane, 0)
    lax.fori_loop(2, 6, along_x, 0)

    def rest(e):
        at = 9 * e
        for row in range(0, 128, STRIP):
            flux_x[at, pl.ds(row, STRIP), :] = local_parts(dens, at + 1, row + 16, STRIP)[2]
        plane(7 * e, 0)
        along_x(6 * e, 0)
        along_x(6 * e + 1, 0)

    def by_parts():
        for j in range(2):
            rim_copy(j).wait_recv()
        for k in range(4):
            from_row(k).wait_recv()

    pl.when(is_first)(lambda: arrived(to_before))
    pl.when(jnp.logical_not(is_first))(lambda: arrived(to_after))
    rest(jnp.where(is_first, 1, 0))
    pl.when(is_end)(by_parts)
    pl.when(jnp.logical_not(is_end))(lambda: arrived(to_before))
    rest(jnp.where(is_first, 0, 1))

    @pl.when(jnp.logical_not(is_first))
    def _():
        for copy in to_before:
            copy.wait_send()

    @pl.when(jnp.logical_not(is_last))
    def _():
        for copy in to_after:
            copy.wait_send()

    @pl.when(in_row & jnp.logical_not(is_end))
    def _():
        across_to_row().wait_send()
        to_taker().wait_send()

    @pl.when(is_end)
    def _():
        for j in range(2):
            rim_copy(j).wait_send()
        for k in range(2):
            across_to_taker(k).wait_send()
        for k in range(4):
            to_row(k).wait_send()


def potential(occupation, live, index, proj, core, orbitals):
    tiles = orbitals.reshape(2, 8, 64, 8, 4, 128).transpose(0, 1, 2, 4, 3, 5).reshape(2, 8, 256, 8, 128)
    core = core.reshape(8, 16, 8, 4, 128).transpose(0, 1, 3, 2, 4).reshape(8, 64, 8, 128)
    both = pltpu.VMEM((2, 4, 33, 4, 8, 128), f32)
    strengths = pltpu.VMEM((8, 128), f32)
    points = pltpu.VMEM((64, 128), i32)
    dma = pltpu.SemaphoreType.DMA
    return pl.pallas_call(
        potential_kernel,
        in_specs=[SM, SM, VM, HBM, HBM, HBM],
        out_specs=VM,
        out_shape=jax.ShapeDtypeStruct((8, 128, 512), f32),
        scratch_shapes=[
            pltpu.VMEM((64, 8, 128), f32),
            pltpu.VMEM((8, 64, 8, 128), f32),
            pltpu.VMEM((2048, 2, 8, 128), f32),
            pltpu.VMEM((256 * STEP, 128), f32),
            pltpu.VMEM((256 * STEP, 128), f32),
            pltpu.VMEM((128, 128), f32),
            pltpu.VMEM((12, 160, 512), f32),
            pltpu.VMEM((10, 128, 512), f32),
            pltpu.VMEM((160, 512), f32),
            both,
            both,
            both,
            pltpu.VMEM((4, 33, 4, 8, 128), f32),
            strengths,
            strengths,
            pltpu.VMEM((2, 8, 128), f32),
            points,
            pltpu.SMEM((64, 128), i32),
            pltpu.VMEM((64, 8, 128), f32),
            points,
            pltpu.VMEM((64, 128), f32),
            pltpu.VMEM((256, 8192), bf16),
            dma((3,)),
            dma((16,)),
            dma((8,)),
            dma((8,)),
            dma((8,)),
            dma((8,)),
            dma((2,)),
            dma((2,)),
            dma((4,)),
            dma((4,)),
            pltpu.VMEM((2, 2, 32, 512), f32),
            pltpu.VMEM((2, 32, 512), f32),
            dma((4,)),
            dma((2,)),
            dma((2,)),
            dma((1,)),
            dma((1,)),
            dma((4,)),
            dma((2,)),
            dma((2,)),
        ],
        compiler_params=pltpu.CompilerParams(
            vmem_limit_bytes=60 * MIB, collective_id=0, has_side_effects=True
        ),
        cost_estimate=pl.CostEstimate(flops=100 * MIB, bytes_accessed=40 * MIB, transcendentals=0),
        name="potential",
    )(occupation, live, index, proj, core, tiles)


def shards(orbitals, occupation, core_density, proj_values, block_index, live_points):
    return potential(
        occupation, live_points, block_index, proj_values, core_density, orbitals
    )


def solution(mesh):
    placed = (
        P("band", "dom", None, None),
        P("band"),
        P("dom", "band", None),
        P("dom", None, None),
        P("dom", None),
        P("dom"),
    )
    return jax.shard_map(
        shards, mesh=mesh, in_specs=placed, out_specs=P("dom", "band", None), check_vma=False
    )
```

```python
import functools
import math

import jax
import jax.numpy as jnp
from jax import lax
from jax.experimental import pallas as pl
from jax.experimental.pallas import tpu as pltpu
from jax.sharding import PartitionSpec as P

f32 = jnp.float32
bf16 = jnp.bfloat16
i32 = jnp.int32

coef_a = 0.75 * (3.0 / math.pi) ** (1.0 / 3.0)
kappa_val = 0.804
mu_val = 0.2195149727645171
s_scale = 4.0 * (3.0 * math.pi**2) ** (2.0 / 3.0)
LOG2E = math.log2(math.e)

MIB = 2**20
GROUP = 264
LOW = 256
HIGH = 260
ACC_ROWS = 16 * GROUP
N_ACC = 8
NT = (((1,), (1,)), ((), ()))
VM = pl.BlockSpec(memory_space=pltpu.VMEM)
SM = pl.BlockSpec(memory_space=pltpu.SMEM)
ANY = pl.BlockSpec(memory_space=pl.ANY)
HBM = pl.BlockSpec(memory_space=pltpu.HBM)


def params(mib):
    return pltpu.CompilerParams(vmem_limit_bytes=mib * MIB)


def local_parts(dens, x, row, count):
    mid = dens[x, pl.ds(row, count), :]
    gy = (dens[x, pl.ds(row + 1, count), :] - dens[x, pl.ds(row - 1, count), :]) * 0.5
    gx = (dens[x + 1, pl.ds(row, count), :] - dens[x - 1, pl.ds(row, count), :]) * 0.5
    gz = (pltpu.roll(mid, 511, 1) - pltpu.roll(mid, 1, 1)) * 0.5
    sigma = gy * gy + gx * gx + gz * gz
    logs = jnp.log(mid)
    cube = jnp.exp2(logs * (LOG2E / 3.0))
    inv_four = jnp.exp2(logs * (-4.0 * LOG2E / 3.0))
    reduced = sigma * (inv_four * inv_four) * (1.0 / s_scale)
    under = 1.0 + (mu_val / kappa_val) * reduced
    inv = pl.reciprocal(under, approx=True)
    inv = inv * (2.0 - under * inv)
    slope = mu_val * inv * inv
    factor = (1.0 + kappa_val) - kappa_val * inv
    e_n = (-4.0 / 3.0 * coef_a) * cube * (factor - 2.0 * reduced * slope)
    twice = (-2.0 * coef_a / s_scale) * inv_four * slope
    return e_n, twice * gy, twice * gx, twice * gz


STRIP = 32


def full_plane(dens, x, flux_y, put):
    for row in (8, 144):
        flux_y[pl.ds(row, 8), :] = local_parts(dens, x, row, 8)[1]
    for row in range(16, 144, STRIP):
        e_n, fy, fx, fz = local_parts(dens, x, row, STRIP)
        flux_y[pl.ds(row, STRIP), :] = fy
        put(row - 16, e_n - (pltpu.roll(fz, 511, 1) - pltpu.roll(fz, 1, 1)) * 0.5, fx)


def minus_y(flux_y, row):
    up = flux_y[pl.ds(row + 17, STRIP), :]
    down = flux_y[pl.ds(row + 15, STRIP), :]
    return (up - down) * 0.5


MESH = pl.DeviceIdType.MESH
STEP = 8
ORDER = (0, 3, 1, 2)


def potential_kernel(
    occupation, live, index, proj_hbm, core_hbm, orb,
    pot_ref,
    proj, core,
    buf, picked_a, picked_b, rims, dens, flux_x, flux_y, keep, send, recv, come, w_mine, w_core, w_come, rows_v, rows, beta, tile_of, row_of, vt,
    rows_sem, load_sem, swap_out, swap_in, far_out, far_in, w_out, w_in, halo_out, halo_in,
    hop1, hop2, hop1_out, hop1_in, hop2_out, hop2_in, hop3_out, hop3_in, rim_out, rim_in,
):
    band = lax.axis_index("band")
    dom = lax.axis_index("dom")
    parity = lax.rem(band, 2)
    z_hi = band // 2
    mate = (band + 1 - 2 * parity, dom)
    opposite = (lax.rem(band + 2, 4), dom)
    after = (band, lax.rem(dom + 1, 32))
    before = (band, lax.rem(dom + 31, 32))

    def loads(gi):
        made = []
        for i in range(2):
            x = 2 * ORDER[gi] + i
            for o in range(2):
                made.append(
                    pltpu.make_async_copy(
                        orb.at[o, x], buf.at[pl.ds(256 * x, 256), o], load_sem.at[4 * gi + 2 * i + o]
                    )
                )
        return made

    for copy in loads(0):
        copy.start()
    core_in = pltpu.make_async_copy(core_hbm, core, rows_sem.at[1])
    proj_in = pltpu.make_async_copy(proj_hbm, proj, rows_sem.at[2])
    core_in.start()
    proj_in.start()
    barrier = pltpu.get_barrier_semaphore()
    spot = lax.rem(dom, 16)
    layer = dom - spot
    in_last = spot >= 12
    lane = jnp.where(in_last, spot - 12, spot)
    in_row = (in_last & (lane != 1)) | ((spot < 4) & (lane != 2))
    row_first = jnp.where(in_last, layer + 12, layer)
    sender = jnp.where(in_last, layer, layer + 15)
    taker = jnp.where(in_last, layer + 15, layer)
    far_first = jnp.where(in_last, layer, layer + 12)
    is_last = spot == 15
    is_first = spot == 0
    is_end = is_last | is_first
    other_layer = (band, lax.rem(dom + 16, 32))

    def greet(partner):
        pl.semaphore_signal(barrier, inc=1, device_id=partner, device_id_type=MESH)

    for partner in (mate, opposite, after, before):
        greet(partner)

    @pl.when(in_row)
    def _():
        greet(other_layer)
        greet((band, sender))

    @pl.when(in_row & jnp.logical_not(is_end))
    def _():
        greet((band, taker))

    far_lanes = (jnp.where(in_last, 0, 3), jnp.where(in_last, 1, 2), jnp.where(in_last, 3, 0))
    near_lanes = (jnp.where(in_last, 2, 1), jnp.where(in_last, 0, 3))

    @pl.when(is_end)
    def _():
        for k in far_lanes:
            greet((band, far_first + k))
        for k in near_lanes:
            greet((band, row_first + k))

    w0 = occupation[0].astype(f32) * 0.001
    w1 = occupation[1].astype(f32) * 0.001

    cell = index[...]
    x = cell >> 18
    y = (cell >> 9) & 511
    c = (cell >> 7) & 3
    rows_v[...] = ((x * 64 + (y >> 3)) * 4 + c) * 16 + (y & 7)
    to_rows = pltpu.make_async_copy(rows_v, rows, rows_sem.at[0])
    to_rows.start()
    own = (y - 128 * band) & 511
    g = x >> 1
    tile = jnp.where(g == 0, 0, jnp.where(g == 3, 1, g + 1)) * 4 + c
    pair = (x & 1) * 2
    rim = tile * 8 + pair + jnp.where(own >= 510, own - 510, own - 124)
    is_rim = (own >= 510) | (own < 130)
    tile_of[...] = jnp.where(own < 128, tile, jnp.where(is_rim, 16, -1))
    row_of[...] = jnp.where(own < 128, (x & 1) * 128 + own, rim).astype(f32)

    def squares(tile, count):
        a = buf[pl.ds(tile, count), 0]
        b = buf[pl.ds(tile, count), 1]
        return w0 * a * a + w1 * b * b

    def fill(ref, gi, near, mine):
        q = 2 * (z_hi if near else 1 - z_hi) + (parity if mine else 1 - parity)
        for i in range(2):
            x = 2 * ORDER[gi] + i

            def body(j, _):
                value = squares(x * 256 + q * 64 + 16 * j, 16)
                if near and mine:
                    value = value + core[x, pl.ds(16 * j, 16)]
                ref[near, gi, pl.ds(16 * i + 4 * j, 4)] = value.reshape(4, 4, 8, 128)
                return 0

            lax.fori_loop(0, 4, body, 0, unroll=2)
            q_low = lax.rem(q + 3, 4)
            own = jnp.where(q_low == band, 1.0, 0.0)
            value = squares(x * 256 + q_low * 64 + 60, 4) + own * core[x, 60:64]
            ref[near, gi, 32, :, 2 * i : 2 * i + 2, :] = value[:, 6:8, :]
            q_high = lax.rem(q + 1, 4)
            own = jnp.where(q_high == band, 1.0, 0.0)
            value = squares(x * 256 + q_high * 64, 4) + own * core[x, 0:4]
            ref[near, gi, 32, :, 4 + 2 * i : 6 + 2 * i, :] = value[:, 0:2, :]

    def swap(near, gi):
        return pltpu.make_async_remote_copy(
            src_ref=send.at[near, gi],
            dst_ref=recv.at[near, gi],
            send_sem=swap_out.at[4 * near + gi],
            recv_sem=swap_in.at[4 * near + gi],
            device_id=mate,
            device_id_type=MESH,
        )

    def across(gi, half):
        part = pl.ds(0, 16) if half == 0 else pl.ds(16, 17)
        return pltpu.make_async_remote_copy(
            src_ref=keep.at[0, gi, part],
            dst_ref=come.at[gi, part],
            send_sem=far_out.at[2 * gi + half],
            recv_sem=far_in.at[2 * gi + half],
            device_id=opposite,
            device_id_type=MESH,
        )

    def add_received(near, gi):
        def body(j, _):
            here = pl.ds(3 * j, 3)
            keep[near, gi, here] = keep[near, gi, here] + recv[near, gi, here]
            return 0

        lax.fori_loop(0, 11, body, 0)

    for gi in range(4):
        for copy in loads(gi):
            copy.wait()
        if gi < 3:
            for copy in loads(gi + 1):
                copy.start()
        if gi == 0:
            core_in.wait()
        fill(send, gi, 0, False)
        if gi == 0:
            pl.semaphore_wait(barrier, jnp.where(is_end, 11, jnp.where(in_row, 7, 4)))
        swap(0, gi).start()
        fill(keep, gi, 0, True)
        fill(send, gi, 1, False)
        swap(1, gi).start()
        if gi > 0:
            fill(keep, gi, 1, True)
        swap(0, gi).wait()
        add_received(0, gi)
        if gi < 2:
            across(gi, 0).start()
        if gi < 1:
            across(gi, 1).start()
            fill(keep, gi, 1, True)

    proj_in.wait()
    flat = buf.reshape(32768, 128)
    sub = lax.broadcasted_iota(i32, (128, 128), 0)
    two = lax.broadcasted_iota(i32, (256, 128), 0) - 2 * lax.broadcasted_iota(i32, (256, 128), 1)
    even = two == 0
    odd = two == 1
    lane_ids = lax.broadcasted_iota(i32, (8, 128), 1)
    to_rows.wait()

    def pick(step, j, picked):
        for k in range(128):
            r = rows[STEP * step + j, k]
            picked[pl.ds(256 * j + 2 * k, 2), :] = flat[pl.ds(r, 2, stride=8), :]

    def project(step, j, picked, total):
        b = STEP * step + j
        hot = jnp.where((index[pl.ds(b, 1), :] & 127) == sub, 1.0, 0.0).astype(bf16)
        g = picked[256 * j : 256 * j + 256]
        g1 = g.astype(bf16)
        g2 = (g - g1.astype(f32)).astype(bf16)
        t = jnp.dot(g1, hot, preferred_element_type=f32) + jnp.dot(g2, hot, preferred_element_type=f32)
        be = jnp.where(lane_ids < live[b], proj[b], 0.0)
        beta[b] = be
        p0 = jnp.sum(jnp.where(even, t, 0.0), axis=0, keepdims=True)
        p1 = jnp.sum(jnp.where(odd, t, 0.0), axis=0, keepdims=True)
        c0 = jnp.sum(be * p0, axis=1, keepdims=True)
        c1 = jnp.sum(be * p1, axis=1, keepdims=True)
        return jnp.where(lane_ids == b, w0 * c0 * c0 + w1 * c1 * c1, total)

    def gather_step(i, total):
        for j in range(STEP):
            pick(2 * i + 1, j, picked_b)
            total = project(2 * i, j, picked_a, total)
        for j in range(STEP):
            pick(jnp.minimum(2 * i + 2, 64 // STEP - 1), j, picked_a)
            total = project(2 * i + 1, j, picked_b, total)
        return total

    for j in range(STEP):
        pick(0, j, picked_a)
    w_mine[...] = lax.fori_loop(0, 32 // STEP, gather_step, jnp.zeros((8, 128), f32))

    def send_w(src, at, target):
        return pltpu.make_async_remote_copy(
            src_ref=src,
            dst_ref=w_come.at[at],
            send_sem=w_out.at[at],
            recv_sem=w_in.at[at],
            device_id=target,
            device_id_type=MESH,
        )

    first = send_w(w_mine, 0, mate)
    first.start()
    for gi in range(2):
        swap(1, gi).wait()
        add_received(1, gi)
    first.wait()
    w_core[...] = w_mine[...] + w_come[0]
    second = send_w(w_core, 1, opposite)
    second.start()
    across(1, 1).start()
    across(2, 0).start()
    for gi in range(2, 4):
        swap(1, gi).wait()
        add_received(1, gi)
    second.wait()
    strengths = w_core[...] + w_come[1]

    def spread_step(i, _):
        for j in range(STEP):
            b = STEP * i + j
            be = beta[b]
            w = jnp.sum(jnp.where(lane_ids == b, strengths, 0.0), axis=1, keepdims=True)
            at = jnp.sum(w * be * be, axis=0, keepdims=True)
            a1 = at.astype(bf16).astype(f32)
            hot = (index[pl.ds(b, 1), :] & 127) == sub
            here = pl.ds(pl.multiple_of(128 * STEP * i, 128 * STEP) + 128 * j, 128)
            vt[0:128, here] = jnp.where(hot, a1, 0.0).astype(bf16)
            vt[128:256, here] = jnp.where(hot, at - a1, 0.0).astype(bf16)
        return 0

    lax.fori_loop(0, 64 // STEP, spread_step, 0)

    def spread_tiles(tiles, count):
        ids = lax.broadcasted_iota(i32, (count, 128), 0).astype(f32).astype(bf16)
        acc = jnp.zeros((count * len(tiles), 256), f32)
        for q in range(8):
            strips = []
            for t in tiles:
                hots = []
                for b in range(8 * q, 8 * q + 8):
                    at = jnp.where(tile_of[b : b + 1, :] == t, row_of[b : b + 1, :], -1.0).astype(bf16)
                    hots.append(jnp.where(at == ids, jnp.ones((), bf16), jnp.zeros((), bf16)))
                strips.append(jnp.concatenate(hots, axis=1))
            acc = acc + lax.dot_general(
                jnp.concatenate(strips, axis=0),
                vt[:, 1024 * q : 1024 * q + 1024],
                NT,
                preferred_element_type=f32,
            )
        return acc[:, :128] + acc[:, 128:]

    rims[...] = spread_tiles((16,), 128)

    def density(gi, arrived):
        at = 2 + 2 * ORDER[gi]

        def columns(half, _):
            both = spread_tiles((4 * gi + 2 * half, 4 * gi + 2 * half + 1), 256)
            for j in range(2):
                c = 2 * half + j
                cols = pl.ds(pl.multiple_of(128 * c, 128), 128)
                sums = keep[1, gi, pl.ds(0, 33), c]
                if arrived:
                    sums = sums + come[gi, pl.ds(0, 33), c]
                body = both[256 * j : 256 * j + 256] + sums[0:32].reshape(256, 128)
                rim = rims[pl.ds(pl.multiple_of((4 * gi + c) * 8, 8), 8), :] + sums[32]
                for i in range(2):
                    dens[at + i, 16:144, cols] = body[128 * i : 128 * i + 128]
                    dens[at + i, 14:16, cols] = rim[2 * i : 2 * i + 2]
                    dens[at + i, 144:146, cols] = rim[4 + 2 * i : 6 + 2 * i]
            return 0

        lax.fori_loop(0, 2, columns, 0)

    def add_arrived(gi):
        at = 2 + 2 * ORDER[gi]

        def columns(c, _):
            cols = pl.ds(pl.multiple_of(128 * c, 128), 128)
            rim = come[gi, 32, c]
            for i in range(2):
                dens[at + i, 16:144, cols] = dens[at + i, 16:144, cols] + come[
                    gi, pl.ds(16 * i, 16), c
                ].reshape(128, 128)
                dens[at + i, 14:16, cols] = dens[at + i, 14:16, cols] + rim[2 * i : 2 * i + 2]
                dens[at + i, 144:146, cols] = dens[at + i, 144:146, cols] + rim[4 + 2 * i : 6 + 2 * i]
            return 0

        lax.fori_loop(0, 4, columns, 0)

    def halo(at, source, target, row, count, partner):
        return pltpu.make_async_remote_copy(
            src_ref=dens.at[source, pl.ds(row, count)],
            dst_ref=dens.at[target, pl.ds(row, count)],
            send_sem=halo_out.at[at],
            recv_sem=halo_in.at[at],
            device_id=partner,
            device_id_type=MESH,
        )

    def wait_far(gi):
        across(gi, 0).wait()
        across(gi, 1).wait()

    def plane(x, _):
        def put(row, value, fx):
            pot_ref[x, pl.ds(row, STRIP), :] = value
            flux_x[x + 1, pl.ds(row, STRIP), :] = fx

        full_plane(dens, x + 2, flux_y, put)
        for row in range(0, 128, STRIP):
            here = pl.ds(row, STRIP)
            pot_ref[x, here, :] = pot_ref[x, here, :] - minus_y(flux_y, row)
        return 0

    def along_x(x, _):
        for row in range(0, 128, STRIP):
            here = pl.ds(row, STRIP)
            pot_ref[x, here, :] = (
                pot_ref[x, here, :] - (flux_x[x + 2, here, :] - flux_x[x, here, :]) * 0.5
            )
        return 0

    def remote(src, dst, out, came, partner):
        return pltpu.make_async_remote_copy(
            src_ref=src,
            dst_ref=dst,
            send_sem=out,
            recv_sem=came,
            device_id=partner,
            device_id_type=MESH,
        )

    def part(plane, k):
        return dens.at[pl.ds(plane, 2), pl.ds(pl.multiple_of(16 + 32 * k, 8), 32)]

    gives = jnp.where(in_last, 8, 2)
    lands = jnp.where(in_last, 10, 0)

    piece = jnp.where(in_last, jnp.where(lane == 2, 2, 3), jnp.where(lane == 1, 2, 3))

    def to_row(k):
        slot = k % 2 if k < 2 else 0
        target = (band, far_first + far_lanes[max(k - 1, 0)])
        return remote(part(gives, k), hop1.at[slot], hop1_out.at[k], hop1_in.at[slot], target)

    def across_to_row():
        return remote(hop1.at[0], hop2, hop2_out.at[0], hop2_in.at[0], other_layer)

    def across_to_taker(k):
        return remote(hop1.at[k], part(lands, k), hop2_out.at[k], hop3_in.at[k], other_layer)

    def to_taker():
        return remote(hop2, part(lands, piece), hop3_out.at[0], hop3_in.at[piece], (band, taker))

    def from_row(k):
        return remote(hop2, part(lands, k), hop3_out.at[0], hop3_in.at[k], (band, taker))

    def rim_copy(j):
        here = pl.ds(8 + 136 * j, 8)
        return remote(
            dens.at[jnp.where(in_last, 9, 2), here],
            dens.at[jnp.where(in_last, 1, 10), here],
            rim_out.at[j],
            rim_in.at[j],
            (band, lax.rem(dom + jnp.where(in_last, 1, 31), 32)),
        )

    def send_by_parts():
        for k in range(4):
            to_row(k).start()
        for j in range(2):
            rim_copy(j).start()

    def start(copies):
        for copy in copies:
            copy.start()

    def arrived(copies):
        for copy in copies:
            copy.wait_recv()

    to_before = [halo(0, 2, 10, 8, 144, before), halo(1, 3, 11, 16, 128, before)]
    to_after = [halo(2, 9, 1, 8, 144, after), halo(3, 8, 0, 16, 128, after)]
    wait_far(0)
    density(0, True)
    across(2, 1).start()
    pl.when(is_first)(send_by_parts)
    pl.when(jnp.logical_not(is_first))(lambda: start(to_before))
    wait_far(1)
    density(1, True)
    across(3, 0).start()
    pl.when(is_last)(send_by_parts)
    pl.when(jnp.logical_not(is_last))(lambda: start(to_after))
    wait_far(2)
    density(2, True)

    across(3, 1).start()
    lax.fori_loop(1, 3, plane, 0)
    density(3, False)

    @pl.when(is_end)
    def _():
        for k in range(2):
            to_row(k).wait_recv()
            across_to_taker(k).start()

    @pl.when(in_row & jnp.logical_not(is_end))
    def _():
        to_row(0).wait_recv()
        across_to_row().start()

    wait_far(3)
    add_arrived(3)
    plane(3, 0)

    @pl.when(in_row & jnp.logical_not(is_end))
    def _():
        across_to_row().wait_recv()
        to_taker().start()

    lax.fori_loop(4, 7, plane, 0)
    lax.fori_loop(2, 6, along_x, 0)

    def rest(e):
        at = 9 * e
        for row in range(0, 128, STRIP):
            flux_x[at, pl.ds(row, STRIP), :] = local_parts(dens, at + 1, row + 16, STRIP)[2]
        plane(7 * e, 0)
        along_x(6 * e, 0)
        along_x(6 * e + 1, 0)

    def by_parts():
        for j in range(2):
            rim_copy(j).wait_recv()
        for k in range(4):
            from_row(k).wait_recv()

    pl.when(is_first)(lambda: arrived(to_before))
    pl.when(jnp.logical_not(is_first))(lambda: arrived(to_after))
    rest(jnp.where(is_first, 1, 0))
    pl.when(is_end)(by_parts)
    pl.when(jnp.logical_not(is_end))(lambda: arrived(to_before))
    rest(jnp.where(is_first, 0, 1))

    @pl.when(jnp.logical_not(is_first))
    def _():
        for copy in to_before:
            copy.wait_send()

    @pl.when(jnp.logical_not(is_last))
    def _():
        for copy in to_after:
            copy.wait_send()

    @pl.when(in_row & jnp.logical_not(is_end))
    def _():
        across_to_row().wait_send()
        to_taker().wait_send()

    @pl.when(is_end)
    def _():
        for j in range(2):
            rim_copy(j).wait_send()
        for k in range(2):
            across_to_taker(k).wait_send()
        for k in range(4):
            to_row(k).wait_send()


def potential(occupation, live, index, proj, core, orbitals):
    tiles = orbitals.reshape(2, 8, 64, 8, 4, 128).transpose(0, 1, 2, 4, 3, 5).reshape(2, 8, 256, 8, 128)
    core = core.reshape(8, 16, 8, 4, 128).transpose(0, 1, 3, 2, 4).reshape(8, 64, 8, 128)
    both = pltpu.VMEM((2, 4, 33, 4, 8, 128), f32)
    strengths = pltpu.VMEM((8, 128), f32)
    points = pltpu.VMEM((64, 128), i32)
    dma = pltpu.SemaphoreType.DMA
    return pl.pallas_call(
        potential_kernel,
        in_specs=[SM, SM, VM, HBM, HBM, HBM],
        out_specs=VM,
        out_shape=jax.ShapeDtypeStruct((8, 128, 512), f32),
        scratch_shapes=[
            pltpu.VMEM((64, 8, 128), f32),
            pltpu.VMEM((8, 64, 8, 128), f32),
            pltpu.VMEM((2048, 2, 8, 128), f32),
            pltpu.VMEM((256 * STEP, 128), f32),
            pltpu.VMEM((256 * STEP, 128), f32),
            pltpu.VMEM((128, 128), f32),
            pltpu.VMEM((12, 160, 512), f32),
            pltpu.VMEM((10, 128, 512), f32),
            pltpu.VMEM((160, 512), f32),
            both,
            both,
            both,
            pltpu.VMEM((4, 33, 4, 8, 128), f32),
            strengths,
            strengths,
            pltpu.VMEM((2, 8, 128), f32),
            points,
            pltpu.SMEM((64, 128), i32),
            pltpu.VMEM((64, 8, 128), f32),
            points,
            pltpu.VMEM((64, 128), f32),
            pltpu.VMEM((256, 8192), bf16),
            dma((3,)),
            dma((16,)),
            dma((8,)),
            dma((8,)),
            dma((8,)),
            dma((8,)),
            dma((2,)),
            dma((2,)),
            dma((4,)),
            dma((4,)),
            pltpu.VMEM((2, 2, 32, 512), f32),
            pltpu.VMEM((2, 32, 512), f32),
            dma((4,)),
            dma((2,)),
            dma((2,)),
            dma((1,)),
            dma((1,)),
            dma((4,)),
            dma((2,)),
            dma((2,)),
        ],
        compiler_params=pltpu.CompilerParams(
            vmem_limit_bytes=60 * MIB, collective_id=0, has_side_effects=True
        ),
        cost_estimate=pl.CostEstimate(flops=100 * MIB, bytes_accessed=40 * MIB, transcendentals=0),
        name="potential",
    )(occupation, live, index, proj, core, tiles)


def shards(orbitals, occupation, core_density, proj_values, block_index, live_points):
    return potential(
        occupation, live_points, block_index, proj_values, core_density, orbitals
    )


def solution(mesh):
    placed = (
        P("band", "dom", None, None),
        P("band"),
        P("dom", "band", None),
        P("dom", None, None),
        P("dom", None),
        P("dom"),
    )
    return jax.shard_map(
        shards, mesh=mesh, in_specs=placed, out_specs=P("dom", "band", None), check_vma=False
    )
```
